256 devices in a mesh: segment: 2 (over core), seq: 128 (over z, x, y).
Axes of the slice: x: 4, y: 4, z: 8, core: 2. Of those that a mesh axis runs over, the one named last changes fastest.
Arguments:
- residual_in: bfloat16 [32768, 2048], P('seq'), may hold values from -6 to 6
- queries: bfloat16 [2, 32768, 2048], P('segment', 'seq'), may hold values from -6 to 6
- keys: bfloat16 [2, 32768, 2048], P('segment', 'seq'), may hold values from -6 to 6
- values: bfloat16 [2, 32768, 2048], P('segment', 'seq'), may hold values from -6 to 6
- head_offset: float32 [2, 16], P('segment'), may hold values from -4 to -2
- head_slope: float32 [2, 16], P('segment'), may hold values from 0.2 to 4
- key_lists: int32 [2, 256, 16, 4], P('segment', 'seq'), may hold values from 0 to 255, as said below
- shard_span: int32 [128], replicated, may hold values from 0 to 127, each once
- out_weight: bfloat16 [2, 2048, 2048], P('segment', 'seq'), may hold values from -0.125 to 0.125
Outputs:
- sections_out: bfloat16 [2, 32768, 2048], P('segment', 'seq')
The draws below stay inside these ranges and needn't reach their ends.
Inputs may be any that keep to these rules, and one draw needn't show every extreme that they name: Entry key_lists[s, b, h, j] names a key block stored on another shard than query block b (block c lies on shard c // 2); the 4 entries of one query block and head lie on 4 different shards; in each section the entries of one shard's query blocks name blocks of any one other shard at most 2 * 1 times, every shard reaches that count for some other shard, and one shard is named that often by every other shard. Each shard number appears once; shard i holds the positions from shard_span[i] * 256 on.
All inputs are finite; a program needn't handle non-finite values.
Results may differ from the reference program's by a relative error of at most 0.015.
Values may be sent and summed in bfloat16 or wider, within the bound.
No kernel may reach another device: no remote copies, remote signals or barrier semaphores. Data moves between devices by JAX's collectives and lax.ppermute only.
A program may use at most 128 MiB of HBM per device.

```python
import math
import jax
import jax.numpy as jnp
from jax import lax

D = 2048
HEADS = 16
DH = 128
BLK = 128
LIST = 4
TOK_DEV = 256
TOKENS = 32768
NB = 256
HD = 2048
N_SEQ = 128


def section_lists(base_key):
    shards = N_SEQ
    per_shard = TOK_DEV // BLK
    item_count = per_shard * HEADS * LIST
    mean_pairs = item_count // shards
    row_count = per_shard * HEADS
    pair_key, spread_key = jax.random.split(base_key)
    pairing = jax.random.permutation(pair_key, shards).astype(jnp.int32)
    owner_ids = jnp.arange(shards, dtype=jnp.int32)
    rank_of = jnp.zeros((shards,), jnp.int32).at[pairing].set(owner_ids)
    pair_of = rank_of // 2
    leading = rank_of % 2 == 0
    source_keys = jax.random.split(spread_key, shards)

    def one_source(source, source_key):
        tilt_key, label_key, row_key, local_key = jax.random.split(source_key, 4)
        tilts = jax.random.randint(tilt_key, (shards // 2,), 0, mean_pairs + 1, dtype=jnp.int32).at[0].set(mean_pairs)
        shift_by = tilts[pair_of]
        counts = jnp.where(leading, mean_pairs + shift_by, mean_pairs - shift_by)
        counts = jnp.where(pair_of == pair_of[source], 2 * mean_pairs, counts)
        counts = jnp.where(owner_ids == source, 0, counts)
        labels = jax.random.permutation(label_key, shards).astype(jnp.int32)
        ordered = counts[labels]
        bounds = jnp.cumsum(ordered)
        place_ids = jnp.arange(item_count, dtype=jnp.int32)
        which_one = jnp.sum((bounds[None, :] <= place_ids[:, None]).astype(jnp.int32), axis=1)
        owner_at = labels[which_one]
        row_order = jax.random.permutation(row_key, row_count).astype(jnp.int32)
        places = jnp.arange(LIST, dtype=jnp.int32)[None, :] * row_count + row_order[:, None]
        chosen = owner_at[places]
        local_block = jax.random.randint(local_key, (row_count, LIST), 0, per_shard, dtype=jnp.int32)
        return chosen * per_shard + local_block
    listed = jax.vmap(one_source)(owner_ids, source_keys)
    return listed.reshape(shards * per_shard, HEADS, LIST)


def draw_key_lists(key, part):
    key = jax.random.fold_in(key, 7)
    first_lists = section_lists(jax.random.fold_in(key, 0))
    second_lists = section_lists(jax.random.fold_in(key, 1))
    return jnp.stack([first_lists, second_lists]).astype(jnp.int32)


def levels(key, extent, cuts, least, top_value):
    def one(dim, blocks):
        steps = jax.random.uniform(jax.random.fold_in(jax.random.fold_in(key, 6), dim), (blocks,), jnp.float32, least / len(cuts), top_value / len(cuts))
        return jnp.repeat(jnp.exp(steps), extent[dim] // blocks).reshape((-1,) + (1,) * (len(extent) - dim - 1))

    loudness = one(*cuts[0])
    for cut in cuts[1:]:
        loudness = loudness * one(*cut)
    return loudness


def scatter_about(stream_key, extent, spread, reach, cuts=(), kind=jnp.bfloat16):
    gain = levels(stream_key, extent, cuts, -0.22, 0.18) if cuts else 1.0
    values = jax.random.normal(stream_key, extent, jnp.float32) * spread * gain
    return jnp.minimum(jnp.maximum(values, -reach), reach).astype(kind)


def setup_inputs(seed: int = 0) -> dict:
    splits = jax.random.split(jax.random.key(seed), 10)
    return {
        "residual_in": scatter_about(splits[0], (TOKENS, D), 1.0, 6.0, ((0, 128),)),
        "queries": scatter_about(splits[1], (2, TOKENS, HD), 1.0, 6.0, ((0, 2), (1, 128))),
        "keys": scatter_about(splits[2], (2, TOKENS, HD), 1.0, 6.0, ((0, 2), (1, 128))),
        "values": scatter_about(splits[3], (2, TOKENS, HD), 1.0, 6.0, ((0, 2), (1, 128))),
        "head_offset": jnp.clip(-4.0 + 2.0 * jax.random.uniform(splits[4], (2, HEADS), jnp.float32) ** levels(splits[4], (2, HEADS), ((0, 2),), -0.2, 0.2), -4.0, -2.0),
        "head_slope": jnp.clip(jnp.exp(math.log(4.0) - 2.9957323 * jax.random.uniform(splits[5], (2, HEADS), jnp.float32) ** levels(splits[5], (2, HEADS), ((0, 2),), -0.2, 0.2)), 0.2, 4.0),
        "key_lists": draw_key_lists(jax.random.fold_in(splits[9], 71), 0),
        "shard_span": jax.random.permutation(splits[7], N_SEQ).astype(jnp.int32),
        "out_weight": scatter_about(splits[8], (2, HD, D), HD ** -0.5, 0.125, ((0, 2), (1, 128))),
    }


def pair_weights(query_rows, key_rows, offsets, slopes, query_pos, key_pos):
    raw_dot = jnp.einsum("...qd,...kd->...qk", query_rows.astype(jnp.float32), key_rows.astype(jnp.float32))
    distance = jnp.abs(query_pos[..., :, None] - key_pos[..., None, :]).astype(jnp.float32) / TOKENS
    scores = raw_dot * (DH ** -0.5) + offsets[..., None, None] - slopes[..., None, None] * distance
    return jax.nn.sigmoid(scores).astype(jnp.bfloat16)


def section_attention(queries, keys, values, offsets, slopes, entries, shard_span):
    per_shard = TOK_DEV // BLK
    key_blocks = keys.reshape(NB, BLK, HEADS, DH).transpose(0, 2, 1, 3)
    value_blocks = values.reshape(NB, BLK, HEADS, DH).transpose(0, 2, 1, 3)
    head_ids = jnp.arange(HEADS, dtype=jnp.int32)[None, :, None]
    rows_in = jnp.arange(TOK_DEV, dtype=jnp.int32)
    block_rows = jnp.arange(BLK, dtype=jnp.int32)

    def one_shard(pieces):
        query_part, key_part, value_part, listed, own_span = pieces
        positions = own_span * TOK_DEV + rows_in
        query_heads = query_part.reshape(TOK_DEV, HEADS, DH).transpose(1, 0, 2)
        key_heads = key_part.reshape(TOK_DEV, HEADS, DH).transpose(1, 0, 2)
        value_head_rows = value_part.reshape(TOK_DEV, HEADS, DH).transpose(1, 0, 2)
        segment_weights = pair_weights(query_heads, key_heads, offsets, slopes, positions, positions)
        segment_output = jnp.einsum("ofg,ogi->ofi", segment_weights.astype(jnp.float32), value_head_rows.astype(jnp.float32))
        picked_keys = key_blocks[listed, head_ids]
        picked_values = value_blocks[listed, head_ids]
        query_sets = query_heads.reshape(HEADS, per_shard, BLK, DH).transpose(1, 0, 2, 3)[:, :, None]
        query_sets = jnp.broadcast_to(query_sets, picked_keys.shape)
        query_pos = positions.reshape(per_shard, 1, 1, BLK)
        key_pos = (shard_span[listed // per_shard] * TOK_DEV + (listed % per_shard) * BLK)[..., None] + block_rows
        pairwise_weight = pair_weights(query_sets, picked_keys, offsets[None, :, None], slopes[None, :, None], query_pos, key_pos)
        partial_value = jnp.einsum("bhlqk,bhlkd->bhlqd", pairwise_weight.astype(jnp.float32), picked_values.astype(jnp.float32)).astype(jnp.bfloat16)
        remote = jnp.sum(partial_value.astype(jnp.float32), axis=2)
        merged = segment_output.reshape(HEADS, per_shard, BLK, DH).transpose(1, 2, 0, 3) + remote.transpose(0, 2, 1, 3)
        return merged.reshape(TOK_DEV, HD).astype(jnp.bfloat16)

    attended = lax.map(one_shard, (queries.reshape(N_SEQ, TOK_DEV, HD), keys.reshape(N_SEQ, TOK_DEV, HD), values.reshape(N_SEQ, TOK_DEV, HD), entries.reshape(N_SEQ, per_shard, HEADS, LIST), shard_span))
    return attended.reshape(TOKENS, HD)


def reference(residual_in, queries, keys, values, head_offset, head_slope, key_lists, shard_span, out_weight):
    projected = []
    for section in range(2):
        attended = section_attention(queries[section], keys[section], values[section], head_offset[section], head_slope[section], key_lists[section], shard_span)
        projected.append(jnp.dot(attended, out_weight[section], preferred_element_type=jnp.float32))
    first_out = (residual_in.astype(jnp.float32) + projected[0]).astype(jnp.bfloat16)
    latter_section = (first_out.astype(jnp.float32) + projected[1]).astype(jnp.bfloat16)
    return jnp.stack([first_out, latter_section])
```

```python
import jax
import jax.numpy as jnp
from jax import lax
from jax.experimental import pallas as pl
from jax.experimental.pallas import tpu as pltpu
from jax.sharding import Mesh, PartitionSpec as P

NZ, NX, NY = 8, 4, 4
PLANE = NX * NY
SEQ = ("z", "x", "y")
CHUNKS = ((0,), (-1, 1), (-2, 2), (-3, 3), (4,))
AHEAD = 3


def pack_kernel(slots, half, sel_ref, *refs):
    sources, out_ref, sem = refs[:-2], refs[-2], refs[-1]

    def copies(i):
        idx = sel_ref[i]
        if half:
            low, high = sources

            @pl.when(idx < half)
            def _():
                pltpu.make_async_copy(low.at[idx], out_ref.at[i], sem).start()

            @pl.when(idx >= half)
            def _():
                pltpu.make_async_copy(high.at[idx - half], out_ref.at[i], sem).start()
        else:
            for n, source in enumerate(sources):

                @pl.when(lax.rem(i // slots, len(sources)) == n)
                def _(source=source):
                    pltpu.make_async_copy(source.at[idx], out_ref.at[i], sem).start()

    total = out_ref.shape[0]

    @pl.loop(0, total)
    def _(i):
        copies(i)

    pltpu.make_async_copy(out_ref, out_ref, sem).wait()


def pack(sel, sources, half=0):
    _, shards, slots = sel.shape
    total = sel.size
    block = sources[0].shape[1:]
    out = pl.pallas_call(
        lambda *refs: pack_kernel(slots, half, *refs),
        out_shape=jax.ShapeDtypeStruct((total,) + block, sources[0].dtype),
        in_specs=[pl.BlockSpec(memory_space=pltpu.SMEM)]
        + [pl.BlockSpec(memory_space=pl.ANY)] * len(sources),
        out_specs=pl.BlockSpec(memory_space=pl.ANY),
        scratch_shapes=[pltpu.SemaphoreType.DMA],
        name="pack_blocks",
    )(sel.reshape(total), *sources)
    return out


def attend_kernel(
    per_shard, listed, scale, chunk_ref, slot_ref, base_ref, offset_ref, slope_ref,
    q_ref, k_ref, v_ref, *refs
):
    got, out_ref, held, sems = refs[:-3], refs[-3], refs[-2], refs[-1]
    h = pl.program_id(0)
    heads = pl.num_programs(0)
    blk = q_ref.shape[0] // per_shard
    items = per_shard * listed
    depth = AHEAD + 1

    def fetch(head):
        place = lax.rem(head, depth)
        for b in range(per_shard):
            for j in range(listed):
                i = (b * heads + head) * listed + j
                for c, buffer in enumerate(got):

                    @pl.when(chunk_ref[i] == c)
                    def _(buffer=buffer, i=i, n=b * listed + j):
                        pltpu.make_async_copy(
                            buffer.at[slot_ref[i]], held.at[place, n], sems.at[place]
                        ).start()

    @pl.when(h == 0)
    def _():
        for ahead in range(AHEAD):
            fetch(jnp.int32(ahead))

    @pl.when(h + AHEAD < heads)
    def _():
        fetch(h + AHEAD)

    offset = offset_ref[h]
    slope = slope_ref[h] / (1.0 * TOTAL)

    def weights(q, k, base):
        raw = lax.dot_general(q, k, (((1,), (1,)), ((), ())), preferred_element_type=jnp.float32)
        rows = lax.broadcasted_iota(jnp.int32, raw.shape, 0)
        cols = lax.broadcasted_iota(jnp.int32, raw.shape, 1)
        distance = jnp.abs(rows - cols + base).astype(jnp.float32)
        score = raw * scale + offset - slope * distance
        return (1.0 / (1.0 + jnp.exp(-score))).astype(jnp.bfloat16)

    local_w = weights(q_ref[...], k_ref[...], 0)
    local = jnp.dot(local_w, v_ref[...], preferred_element_type=jnp.float32)
    place = lax.rem(h, depth)
    pltpu.make_async_copy(held.at[place], held.at[place], sems.at[place]).wait()
    for b in range(per_shard):
        q = q_ref[b * blk:(b + 1) * blk, :]
        total = local[b * blk:(b + 1) * blk, :]
        for j in range(listed):
            i = (b * heads + h) * listed + j
            n = b * listed + j
            w = weights(q, held[place, n, 0], base_ref[i])
            total += jnp.dot(w, held[place, n, 1], preferred_element_type=jnp.float32)
        out_ref[b * blk:(b + 1) * blk, :] = total.astype(out_ref.dtype)


TOTAL = 32768


def attend(chunk, slot, base, offsets, slopes, q, k, v, got, per_shard, listed):
    tokens, width = q.shape
    heads = offsets.shape[0]
    head_size = width // heads
    blk = tokens // per_shard
    column = pl.BlockSpec((tokens, head_size), lambda h: (0, h))
    smem = pl.BlockSpec(memory_space=pltpu.SMEM)
    return pl.pallas_call(
        lambda *refs: attend_kernel(per_shard, listed, head_size ** (-0.5), *refs),
        grid=(heads,),
        out_shape=jax.ShapeDtypeStruct((tokens, width), jnp.bfloat16),
        in_specs=[smem] * 5 + [column] * 3 + [pl.BlockSpec(memory_space=pl.ANY)] * len(got),
        out_specs=column,
        scratch_shapes=[
            pltpu.VMEM((AHEAD + 1, per_shard * listed, 2, blk, head_size), jnp.bfloat16),
            pltpu.SemaphoreType.DMA((AHEAD + 1,)),
        ],
        compiler_params=pltpu.CompilerParams(vmem_limit_bytes=32 * 1024 * 1024),
        name="attend",
    )(chunk, slot, base, offsets, slopes, q, k, v, *got)


def per_device(
    residual_in, queries, keys, values, head_offset, head_slope, key_lists, shard_span, out_weight
):
    q, k, v = queries[0], keys[0], values[0]
    offsets, slopes, entries = head_offset[0], head_slope[0], key_lists[0]
    per_shard, heads, listed = entries.shape
    tokens, width = q.shape
    head_size = width // heads
    blk = tokens // per_shard
    rows = per_shard * heads
    items = rows * listed
    slots = 2
    my_z = lax.axis_index("z")
    my_p = lax.axis_index("x") * NY + lax.axis_index("y")

    def blocked(a):
        return a.reshape(per_shard, blk, heads, head_size).transpose(0, 2, 1, 3)

    kv = jnp.stack([blocked(k), blocked(v)], axis=2).reshape(rows, 2, blk, head_size)

    up = [(i, (i + 1) % NZ) for i in range(NZ)]
    down = [(i, (i - 1) % NZ) for i in range(NZ)]
    shards = {0: kv}
    a = b = kv
    for n in (1, 2, 3):
        a, b = lax.ppermute(a, "z", up), lax.ppermute(b, "z", down)
        shards[-n], shards[n] = a, b
    half = rows // 2
    far = (lax.ppermute(a[:half], "z", up), lax.ppermute(b[half:], "z", down))

    mine = entries.reshape(items)
    asked = lax.all_gather(mine, ("x", "y"), axis=0)
    item_ids = jnp.arange(items, dtype=jnp.int32)
    item_head = item_ids // listed % heads

    def ranks(owner):
        earlier = item_ids[:, None] > item_ids[None, :]
        same = owner[..., :, None] == owner[..., None, :]
        return jnp.sum((same & earlier).astype(jnp.int32), axis=-1)

    asked_owner = asked // per_shard
    asked_rank = ranks(asked_owner)
    asked_block = asked % per_shard * heads + item_head

    def selection(dz):
        z = (my_z + dz) % NZ
        here = (asked_owner == z * PLANE + my_p)[:, None, :] & (
            asked_rank[:, None, :] == jnp.arange(slots, dtype=jnp.int32)[None, :, None]
        )
        return jnp.sum(jnp.where(here, asked_block[:, None, :], 0), axis=-1)

    got = []
    for chunk in CHUNKS:
        sel = jnp.stack([selection(dz) for dz in chunk], axis=1)
        if chunk == (4,):
            sent = pack(sel, far, half)
        else:
            sent = pack(sel, [shards[dz] for dz in chunk])
        got.append(lax.all_to_all(sent, ("x", "y"), split_axis=0, concat_axis=0, tiled=True))

    owner = mine // per_shard
    rank = ranks(owner)
    dz = (owner // PLANE - my_z) % NZ
    chunk_of = jnp.minimum(dz, NZ - dz)
    count = jnp.where((dz == 0) | (dz == 4), 1, 2)
    within = jnp.where((dz > 0) & (dz < 4), 1, 0)
    slot_of = (owner % PLANE * count + within) * slots + rank
    own_span = shard_span[my_z * PLANE + my_p]
    query_at = own_span * tokens + item_ids // (heads * listed) * blk
    key_at = shard_span[owner] * tokens + mine % per_shard * blk
    base = query_at - key_at

    weight = lax.all_gather(out_weight[0], ("x", "y"), axis=0, tiled=True)
    weight, _ = lax.optimization_barrier((weight, far))
    weight = lax.all_gather(weight, "z", axis=0, tiled=True)

    attended = attend(
        chunk_of, slot_of, base, offsets, slopes, q, k, v, got, per_shard, listed
    )
    projected = jnp.dot(attended, weight, preferred_element_type=jnp.float32)
    first_out = (residual_in.astype(jnp.float32) + projected).astype(jnp.bfloat16)
    handed = lax.ppermute(first_out, "segment", [(0, 1)])
    latter = (handed.astype(jnp.float32) + projected).astype(jnp.bfloat16)
    return jnp.where(lax.axis_index("segment") == 0, first_out, latter)[None]


def solution(mesh):
    fine = Mesh(mesh.devices.reshape(2, NZ, NX, NY), ("segment",) + SEQ)
    in_specs = (
        P(SEQ, None),
        P("segment", SEQ, None),
        P("segment", SEQ, None),
        P("segment", SEQ, None),
        P("segment", None),
        P("segment", None),
        P("segment", SEQ, None, None),
        P(),
        P("segment", SEQ, None),
    )
    return jax.shard_map(
        per_device, mesh=fine, in_specs=in_specs, out_specs=P("segment", SEQ, None), check_vma=False
    )
```

```python
import jax
import jax.numpy as jnp
from jax import lax
from jax.experimental import pallas as pl
from jax.experimental.pallas import tpu as pltpu
from jax.sharding import Mesh, PartitionSpec as P

NZ, NX, NY = 8, 4, 4
PLANE = NX * NY
SEQ = ("z", "x", "y")
CHUNKS = ((0,), (-1, 1), (-2, 2), (-3, 3), (4,))
ORDER = sum(CHUNKS, ())


def pack_kernel(slots, half, sel_ref, *refs):
    sources, out_ref, sem = refs[:-2], refs[-2], refs[-1]

    def copy(source, idx, i):
        pltpu.make_async_copy(source.at[idx], out_ref.at[i], sem).start()

    @pl.loop(0, out_ref.shape[0] // (slots * (1 if half else len(sources))))
    def _(p):
        if half:
            low, high = sources
            for s in range(slots):
                i = p * slots + s
                idx = sel_ref[i]

                @pl.when(idx < half)
                def _(idx=idx, i=i):
                    copy(low, idx, i)

                @pl.when(idx >= half)
                def _(idx=idx, i=i):
                    copy(high, idx - half, i)
        else:
            for n, source in enumerate(sources):
                for s in range(slots):
                    i = (p * len(sources) + n) * slots + s
                    copy(source, sel_ref[i], i)

    pltpu.make_async_copy(out_ref, out_ref, sem).wait()


def pack(sel, sources, half=0):
    slots = sel.shape[-1]
    total = sel.size
    block = sources[0].shape[1:]
    moved = 2 * total * block[0] * block[1] * block[2] * 2
    return pl.pallas_call(
        lambda *refs: pack_kernel(slots, half, *refs),
        out_shape=jax.ShapeDtypeStruct((total,) + block, sources[0].dtype),
        in_specs=[pl.BlockSpec(memory_space=pltpu.SMEM)]
        + [pl.BlockSpec(memory_space=pltpu.VMEM)] * len(sources),
        out_specs=pl.BlockSpec(memory_space=pl.ANY),
        scratch_shapes=[pltpu.SemaphoreType.DMA],
        compiler_params=pltpu.CompilerParams(vmem_limit_bytes=24 * 1024 * 1024),
        cost_estimate=pl.CostEstimate(flops=0, bytes_accessed=moved, transcendentals=0),
        name="pack_blocks",
    )(sel.reshape(total), *sources)


LOG2E = 1.4426950408889634


def local_kernel(scale, offset_ref, slope_ref, q_ref, k_ref, v_ref, out_ref):
    h = pl.program_id(0)
    raw = lax.dot_general(
        q_ref[...], k_ref[...], (((1,), (1,)), ((), ())), preferred_element_type=jnp.float32
    )
    rows = lax.broadcasted_iota(jnp.int32, raw.shape, 0)
    cols = lax.broadcasted_iota(jnp.int32, raw.shape, 1)
    distance = jnp.abs(rows - cols).astype(jnp.float32)
    power = raw * (-scale * LOG2E) + (distance * slope_ref[h] - offset_ref[h])
    w = (1.0 / (1.0 + jnp.exp2(power))).astype(jnp.bfloat16)
    out_ref[...] = jnp.dot(w, v_ref[...], preferred_element_type=jnp.float32)


def local_part(offsets, slopes, q, k, v, heads):
    tokens, width = q.shape
    head_size = width // heads
    column = pl.BlockSpec((tokens, head_size), lambda h: (0, h))
    smem = pl.BlockSpec(memory_space=pltpu.SMEM)
    return pl.pallas_call(
        lambda *refs: local_kernel(head_size ** (-0.5), *refs),
        grid=(heads,),
        out_shape=jax.ShapeDtypeStruct((tokens, width), jnp.float32),
        in_specs=[smem] * 2 + [column] * 3,
        out_specs=column,
        cost_estimate=pl.CostEstimate(
            flops=4 * tokens * tokens * width, bytes_accessed=10 * tokens * width,
            transcendentals=2 * heads * tokens * tokens,
        ),
        name="local_part",
    )(offsets, slopes, q, k, v)


GROUP = 4


def listed_kernel(
    scale, heads, listed, item_ref, near_ref, far_ref, q_ref, got_ref, acc_ref, out_ref, total
):
    step = pl.program_id(0)
    blk, head_size = got_ref.shape[2:]

    @pl.when(step == 0)
    def _():
        total[...] = acc_ref[...]

    found = [item_ref[step * GROUP + n] for n in range(GROUP)]
    some = found[0]
    for item in found[1:]:
        some = some + item

    @pl.when(some > 0)
    def _():
        rows = lax.broadcasted_iota(jnp.int32, (blk, blk), 0)
        cols = lax.broadcasted_iota(jnp.int32, (blk, blk), 1)
        apart = (rows - cols).astype(jnp.float32)
        parts = []
        for n, item in enumerate(found):
            i = jnp.maximum(item - 1, 0)
            row, head = i // (heads * listed), lax.rem(i // listed, heads)
            at = (
                pl.ds(pl.multiple_of(row * blk, blk), blk),
                pl.ds(pl.multiple_of(head * head_size, head_size), head_size),
            )
            raw = lax.dot_general(
                q_ref[at], got_ref[n, 0], (((1,), (1,)), ((), ())),
                preferred_element_type=jnp.float32,
            )
            power = raw * (-scale * LOG2E) + (apart * far_ref[i] + near_ref[i])
            w = (1.0 / (1.0 + jnp.exp2(power))).astype(jnp.bfloat16)
            parts.append((item, at, jnp.dot(w, got_ref[n, 1], preferred_element_type=jnp.float32)))
        for item, at, part in parts:

            @pl.when(item > 0)
            def _(at=at, part=part):
                total[at] += part

    @pl.when(step == pl.num_programs(0) - 1)
    def _():
        out_ref[...] = total[...].astype(out_ref.dtype)


def listed_part(found, near, far, q, got, acc, heads, listed, dtype):
    slots = got.shape[0]
    tokens, width = q.shape
    blk, head_size = got.shape[2:]
    smem = pl.BlockSpec(memory_space=pltpu.SMEM)
    whole = pl.BlockSpec((tokens, width), lambda n: (0, 0))
    return pl.pallas_call(
        lambda *refs: listed_kernel(head_size ** (-0.5), heads, listed, *refs),
        grid=(slots // GROUP,),
        out_shape=jax.ShapeDtypeStruct((tokens, width), dtype),
        in_specs=[smem] * 3
        + [whole, pl.BlockSpec((GROUP,) + got.shape[1:], lambda n: (n, 0, 0, 0)), whole],
        out_specs=whole,
        scratch_shapes=[pltpu.VMEM((tokens, width), jnp.float32)],
        compiler_params=pltpu.CompilerParams(vmem_limit_bytes=32 * 1024 * 1024),
        cost_estimate=pl.CostEstimate(
            flops=4 * slots * blk * blk * head_size, bytes_accessed=got.size * 2 + 10 * q.size,
            transcendentals=2 * slots * blk * blk,
        ),
        name="listed_part",
    )(found, near, far, q, got, acc)


def ring_steps(block, axis):
    size = lax.axis_size(axis)
    up = [(i, (i + 1) % size) for i in range(size)]
    down = [(i, (i - 1) % size) for i in range(size)]
    held = {0: block}
    a = b = block
    for n in range(1, size // 2):
        a, b = lax.ppermute(a, axis, up), lax.ppermute(b, axis, down)
        held[-n], held[n] = a, b
    half = block.shape[0] // 2
    held[size // 2] = jnp.concatenate(
        [lax.ppermute(a[:half], axis, up), lax.ppermute(b[half:], axis, down)]
    )
    return held


def ring_gather(block, axis):
    size = lax.axis_size(axis)
    at = lax.axis_index(axis)
    out = jnp.zeros((size,) + block.shape, block.dtype)
    for n, part in ring_steps(block, axis).items():
        out = lax.dynamic_update_index_in_dim(out, part, (at + n) % size, 0)
    return out.reshape((size * block.shape[0],) + block.shape[1:])


def after(x, *others):
    return lax.optimization_barrier((x, others))[0]


def per_device(
    residual_in, queries, keys, values, head_offset, head_slope, key_lists, shard_span, out_weight
):
    q, k, v = queries[0], keys[0], values[0]
    offsets, slopes, entries = head_offset[0], head_slope[0], key_lists[0]
    per_shard, heads, listed = entries.shape
    tokens, width = q.shape
    head_size = width // heads
    blk = tokens // per_shard
    rows = per_shard * heads
    items = rows * listed
    slots = 2
    my_z = lax.axis_index("z")
    my_p = lax.axis_index("x") * NY + lax.axis_index("y")

    def blocked(a):
        return a.reshape(per_shard, blk, heads, head_size).transpose(0, 2, 1, 3)

    kv = jnp.stack([blocked(k), blocked(v)], axis=2).reshape(rows, 2, blk, head_size)

    mine = entries.reshape(items)
    asked = lax.all_gather(mine, ("x", "y"), axis=0)
    item_ids = jnp.arange(items, dtype=jnp.int32)
    item_head = item_ids // listed % heads

    def ranks(owner):
        earlier = item_ids[:, None] > item_ids[None, :]
        same = owner[..., :, None] == owner[..., None, :]
        return jnp.sum((same & earlier).astype(jnp.int32), axis=-1)

    asked_owner = asked // per_shard
    asked_rank = ranks(asked_owner)
    asked_block = asked % per_shard * heads + item_head

    zs = (my_z + jnp.array(ORDER, jnp.int32)) % NZ
    slot_ids = jnp.arange(slots, dtype=jnp.int32)
    here = (asked_owner[:, None, None, :] == (zs * PLANE + my_p)[None, :, None, None]) & (
        asked_rank[:, None, None, :] == slot_ids[None, None, :, None]
    )
    selected = jnp.sum(jnp.where(here, asked_block[:, None, None, :], 0), axis=-1)

    owner = mine // per_shard
    rank = ranks(owner)
    own_span = shard_span[my_z * PLANE + my_p]
    query_at = own_span * tokens + item_ids // (heads * listed) * blk
    key_at = shard_span[owner] * tokens + mine % per_shard * blk
    base = (query_at - key_at).astype(jnp.float32)
    slope = slopes * (LOG2E / (tokens * NZ * PLANE))
    offset = offsets * LOG2E
    def by_item(a):
        return jnp.broadcast_to(a[None, :, None], (per_shard, heads, listed)).reshape(items)

    far_item = jnp.where(base > 0, 1.0, -1.0) * by_item(slope)
    near_item = far_item * base - by_item(offset)
    here = (
        (owner // PLANE == zs[None, :, None, None])
        & (owner % PLANE == jnp.arange(PLANE, dtype=jnp.int32)[:, None, None, None])
        & (rank == slot_ids[None, None, :, None])
    )
    found = jnp.sum(jnp.where(here, item_ids + 1, 0), axis=-1)
    selected, found, near_item, far_item = lax.optimization_barrier(
        (selected, found, near_item, far_item)
    )

    def part_of(table, n):
        first = sum(len(chunk) for chunk in CHUNKS[:n])
        return table[:, first:first + len(CHUNKS[n])]

    up = [(i, (i + 1) % NZ) for i in range(NZ)]
    down = [(i, (i - 1) % NZ) for i in range(NZ)]
    half = rows // 2

    def served(sent):
        return lax.all_to_all(sent, ("x", "y"), split_axis=0, concat_axis=0, tiled=True)

    def chosen(n, *sources, cut=0):
        return pack(part_of(selected, n), sources, cut)

    def added(n, got, acc, dtype=jnp.float32):
        slot_items = part_of(found, n).reshape(-1)
        return listed_part(
            slot_items, near_item, far_item, q, got, acc, heads, listed, dtype
        )

    def step(pair):
        return lax.ppermute(pair[0], "z", up), lax.ppermute(pair[1], "z", down)

    ring = step((kv, kv))
    got = served(chosen(0, kv))
    weight = ring_gather(ring_gather(out_weight[0], "y"), "x")
    acc = local_part(offset, slope, q, k, v, heads)
    ring = after(ring, got, acc, weight)
    for n in (1, 2, 3):
        later = step(ring) if n < 3 else step((ring[0][:half], ring[1][half:]))
        sent = after(chosen(n, *ring), got)
        acc = added(n - 1, got, after(acc, sent))
        got = served(sent)
        ring = after(later, acc)
    whole_weight = lax.all_gather(after(weight, ring), "z", axis=0, tiled=True)
    sent = after(chosen(4, *ring, cut=half), got)
    acc = added(3, got, after(acc, sent))
    attended = added(4, served(sent), acc, jnp.bfloat16)

    first, latter = [], []
    cut = width // 2
    for n in range(2):
        columns = slice(n * cut, (n + 1) * cut)
        projected = jnp.dot(attended, whole_weight[:, columns], preferred_element_type=jnp.float32)
        first.append((residual_in[:, columns].astype(jnp.float32) + projected).astype(jnp.bfloat16))
        handed = lax.ppermute(first[-1], "segment", [(0, 1)])
        latter.append((handed.astype(jnp.float32) + projected).astype(jnp.bfloat16))
    first, latter = jnp.concatenate(first, axis=1), jnp.concatenate(latter, axis=1)
    return jnp.where(lax.axis_index("segment") == 0, first, latter)[None]


def solution(mesh):
    fine = Mesh(mesh.devices.reshape(2, NZ, NX, NY), ("segment",) + SEQ)
    in_specs = (
        P(SEQ, None),
        P("segment", SEQ, None),
        P("segment", SEQ, None),
        P("segment", SEQ, None),
        P("segment", None),
        P("segment", None),
        P("segment", SEQ, None, None),
        P(),
        P("segment", SEQ, None),
    )
    return jax.shard_map(
        per_device, mesh=fine, in_specs=in_specs, out_specs=P("segment", SEQ, None), check_vma=False
    )
```

```python
import jax
import jax.numpy as jnp
from jax import lax
from jax.experimental import pallas as pl
from jax.experimental.pallas import tpu as pltpu
from jax.sharding import Mesh, PartitionSpec as P

NZ, NX, NY = 8, 4, 4
PLANE = NX * NY
SEQ = ("z", "x", "y")
CHUNKS = ((0,), (-1, 1), (-2, 2), (-3, 3), (4,))
ORDER = sum(CHUNKS, ())
LIGHT = pl.CostEstimate(flops=1, bytes_accessed=1, transcendentals=0)
HEAVY = pl.CostEstimate(flops=50_000_000_000, bytes_accessed=150_000_000, transcendentals=0)


def pack_kernel(slots, half, extra, sel_ref, *refs):
    sources, out_ref, sem = refs[:-2], refs[-2], refs[-1]
    if extra:
        sources, extra_ref = sources[:-1], sources[-1]
    shards = 1 if half else len(sources)
    per_place = shards * slots + extra

    def copy(source, i):
        pltpu.make_async_copy(source, out_ref.at[i], sem).start()

    @pl.loop(0, PLANE)
    def _(p):
        for n in range(shards):
            for s in range(slots):
                i = p * per_place + n * slots + s
                idx = sel_ref[(p * shards + n) * slots + s]
                if half:

                    @pl.when(idx < half)
                    def _(idx=idx, i=i):
                        copy(sources[0].at[idx], i)

                    @pl.when(idx >= half)
                    def _(idx=idx, i=i):
                        copy(sources[1].at[idx - half], i)
                else:
                    copy(sources[n].at[idx], i)
        if extra:
            copy(extra_ref, p * per_place + per_place - 1)

    pltpu.make_async_copy(out_ref, out_ref, sem).wait()


def pack(sel, sources, half=0, extra=None):
    slots = sel.shape[-1]
    block = sources[0].shape[1:]
    extras = [] if extra is None else [extra]
    total = sel.size + PLANE * len(extras)
    return pl.pallas_call(
        lambda *refs: pack_kernel(slots, half, len(extras), *refs),
        out_shape=jax.ShapeDtypeStruct((total,) + block, sources[0].dtype),
        in_specs=[pl.BlockSpec(memory_space=pltpu.SMEM)]
        + [pl.BlockSpec(memory_space=pltpu.VMEM)] * (len(sources) + len(extras)),
        out_specs=pl.BlockSpec(memory_space=pl.ANY),
        scratch_shapes=[pltpu.SemaphoreType.DMA],
        compiler_params=pltpu.CompilerParams(vmem_limit_bytes=24 * 1024 * 1024),
        cost_estimate=HEAVY,
        name="pack_blocks",
    )(sel.reshape(sel.size), *sources, *extras)


LOG2E = 1.4426950408889634


def local_kernel(scale, offset_ref, slope_ref, q_ref, k_ref, v_ref, out_ref):
    h = pl.program_id(0)
    raw = lax.dot_general(
        q_ref[...], k_ref[...], (((1,), (1,)), ((), ())), preferred_element_type=jnp.float32
    )
    rows = lax.broadcasted_iota(jnp.int32, raw.shape, 0)
    cols = lax.broadcasted_iota(jnp.int32, raw.shape, 1)
    distance = jnp.abs(rows - cols).astype(jnp.float32)
    power = raw * (-scale * LOG2E) + (distance * slope_ref[h] - offset_ref[h])
    w = (1.0 / (1.0 + jnp.exp2(power))).astype(jnp.bfloat16)
    out_ref[...] = jnp.dot(w, v_ref[...], preferred_element_type=jnp.float32)


def local_part(offsets, slopes, q, k, v, heads):
    tokens, width = q.shape
    head_size = width // heads
    column = pl.BlockSpec((tokens, head_size), lambda h: (0, h))
    smem = pl.BlockSpec(memory_space=pltpu.SMEM)
    return pl.pallas_call(
        lambda *refs: local_kernel(head_size ** (-0.5), *refs),
        grid=(heads,),
        out_shape=jax.ShapeDtypeStruct((tokens, width), jnp.float32),
        in_specs=[smem] * 2 + [column] * 3,
        out_specs=column,
        cost_estimate=LIGHT,
        name="local_part",
    )(offsets, slopes, q, k, v)


GROUP = 8


def listed_kernel(
    scale, heads, listed, order_ref, bound_ref, slot_ref, near_ref, far_ref, q_ref, got_ref,
    acc_ref, out_ref, total
):
    blk, head_size = got_ref.shape[2:]
    items = order_ref.shape[0]
    begin, end = bound_ref[0], bound_ref[1]
    total[...] = acc_ref[...]

    @pl.loop(0, (end - begin + GROUP - 1) // GROUP)
    def _(group):
        rows = lax.broadcasted_iota(jnp.int32, (blk, blk), 0)
        cols = lax.broadcasted_iota(jnp.int32, (blk, blk), 1)
        apart = (rows - cols).astype(jnp.float32)
        parts = []
        for n in range(GROUP):
            at_order = begin + group * GROUP + n
            i = order_ref[jnp.minimum(at_order, items - 1)]
            slot = jnp.minimum(slot_ref[i], got_ref.shape[0] - 1)
            row, head = i // (heads * listed), lax.rem(i // listed, heads)
            at = (
                pl.ds(pl.multiple_of(row * blk, blk), blk),
                pl.ds(pl.multiple_of(head * head_size, head_size), head_size),
            )
            raw = lax.dot_general(
                q_ref[at], got_ref[slot, 0], (((1,), (1,)), ((), ())),
                preferred_element_type=jnp.float32,
            )
            power = raw * (-scale * LOG2E) + (apart * far_ref[i] + near_ref[i])
            w = (1.0 / (1.0 + jnp.exp2(power))).astype(jnp.bfloat16)
            part = jnp.dot(w, got_ref[slot, 1], preferred_element_type=jnp.float32)
            parts.append((at_order, at, part))
        for at_order, at, part in parts:

            @pl.when(at_order < end)
            def _(at=at, part=part):
                total[at] += part

    out_ref[...] = total[...].astype(out_ref.dtype)


def listed_part(order, bounds, slot, near, far, q, got, acc, heads, listed, dtype):
    tokens, width = q.shape
    smem = pl.BlockSpec(memory_space=pltpu.SMEM)
    vmem = pl.BlockSpec(memory_space=pltpu.VMEM)
    return pl.pallas_call(
        lambda *refs: listed_kernel((width // heads) ** (-0.5), heads, listed, *refs),
        out_shape=jax.ShapeDtypeStruct((tokens, width), dtype),
        in_specs=[smem] * 5 + [vmem] * 3,
        out_specs=vmem,
        scratch_shapes=[pltpu.VMEM((tokens, width), jnp.float32)],
        compiler_params=pltpu.CompilerParams(vmem_limit_bytes=32 * 1024 * 1024),
        cost_estimate=LIGHT,
        name="listed_part",
    )(order, bounds, slot, near, far, q, got, acc)


def after(x, *others):
    return lax.optimization_barrier((x, others))[0]


def per_device(
    residual_in, queries, keys, values, head_offset, head_slope, key_lists, shard_span, out_weight
):
    q, k, v = queries[0], keys[0], values[0]
    offsets, slopes, entries = head_offset[0], head_slope[0], key_lists[0]
    per_shard, heads, listed = entries.shape
    tokens, width = q.shape
    head_size = width // heads
    blk = tokens // per_shard
    rows = per_shard * heads
    items = rows * listed
    slots = 2
    my_z = lax.axis_index("z")
    my_p = lax.axis_index("x") * NY + lax.axis_index("y")

    def blocked(a):
        return a.reshape(per_shard, blk, heads, head_size).transpose(0, 2, 1, 3)

    kv = jnp.stack([blocked(k), blocked(v)], axis=2).reshape(rows, 2, blk, head_size)

    mine = after(entries, kv).reshape(items)
    item_ids = jnp.arange(items, dtype=jnp.int32)
    owner = mine // per_shard
    earlier = item_ids[:, None] > item_ids[None, :]
    rank = jnp.sum((earlier & (owner[:, None] == owner[None, :])).astype(jnp.int32), axis=-1)
    zs = (my_z + jnp.array(ORDER, jnp.int32)) % NZ
    slot_ids = jnp.arange(slots, dtype=jnp.int32)
    here = (
        (owner // PLANE == zs[None, :, None, None])
        & (owner % PLANE == jnp.arange(PLANE, dtype=jnp.int32)[:, None, None, None])
        & (rank == slot_ids[None, None, :, None])
    )
    block_ids = mine % per_shard * heads + item_ids // listed % heads
    wanted = jnp.sum(jnp.where(here, block_ids, 0), axis=-1)
    selected = lax.all_to_all(wanted, ("x", "y"), split_axis=0, concat_axis=0, tiled=True)

    own_span = shard_span[my_z * PLANE + my_p]
    query_at = own_span * tokens + item_ids // (heads * listed) * blk
    key_at = shard_span[owner] * tokens + mine % per_shard * blk
    base = (query_at - key_at).astype(jnp.float32)
    slope = slopes * (LOG2E / (tokens * NZ * PLANE))
    offset = offsets * LOG2E
    def by_item(a):
        return jnp.broadcast_to(a[None, :, None], (per_shard, heads, listed)).reshape(items)

    far_item = jnp.where(base > 0, 1.0, -1.0) * by_item(slope)
    near_item = far_item * base - by_item(offset)
    dz = (owner // PLANE - my_z) % NZ
    chunk = jnp.minimum(dz, NZ - dz)
    pair = (chunk > 0) & (chunk < len(CHUNKS) - 1)
    shard = jnp.where(pair, owner % PLANE * 2 + (dz < NZ // 2), owner % PLANE)
    slot = shard * jnp.where(chunk == 0, slots + 1, slots) + rank
    ahead = (chunk[:, None] < chunk[None, :]) | (
        (chunk[:, None] == chunk[None, :]) & (item_ids[:, None] < item_ids[None, :])
    )
    turn = jnp.sum(ahead.astype(jnp.int32), axis=0)
    order = jnp.sum(jnp.where(turn[:, None] == item_ids[None, :], item_ids[:, None], 0), axis=0)
    edges = jnp.arange(len(CHUNKS) + 1, dtype=jnp.int32)
    edges = jnp.sum((chunk[None, :] < edges[:, None]).astype(jnp.int32), axis=1)

    def part_of(table, n):
        first = sum(len(chunk) for chunk in CHUNKS[:n])
        return table[:, first:first + len(CHUNKS[n])]

    up = [(i, (i + 1) % NZ) for i in range(NZ)]
    down = [(i, (i - 1) % NZ) for i in range(NZ)]
    half = rows // 2

    def served(sent):
        return lax.all_to_all(sent, ("x", "y"), split_axis=0, concat_axis=0, tiled=True)

    def chosen(n, *sources, cut=0, extra=None):
        return pack(part_of(selected, n), sources, cut, extra)

    def added(n, got, acc, dtype=jnp.float32):
        bounds = edges[n:n + 2]
        return listed_part(
            order, bounds, slot, near_item, far_item, q, got, acc, heads, listed, dtype
        )

    def step(pair):
        return lax.ppermute(pair[0], "z", up), lax.ppermute(pair[1], "z", down)

    ring = step((kv, kv))
    packed = chosen(0, kv, extra=out_weight.reshape(kv.shape[1:]))
    got = served(packed)
    acc = local_part(offset, slope, q, k, v, heads)
    ring = after(ring, packed, acc)
    for n in (1, 2, 3):
        later = step(ring) if n < 3 else step((ring[0][:half], ring[1][half:]))
        packed = chosen(n, *ring)
        if n > 1:
            acc = added(n - 2, before, after(acc, packed))
        else:
            weight = got.reshape((PLANE, slots + 1) + kv.shape[1:])[:, slots]
            weight = weight.reshape(-1, width)
        if n == 3:
            later = after(later, acc)
            packed = after(packed, later)
        before, sent = got, after(packed, got)
        got = served(sent)
        ring = after(later, sent, acc)
    weight = lax.all_gather(after(weight, ring), "z", axis=0, tiled=True)
    packed = chosen(4, *ring, cut=half)
    acc = added(2, before, after(acc, packed))
    sent = after(packed, got, acc)
    acc = added(3, got, after(acc, sent))
    attended = added(4, served(sent), acc, jnp.bfloat16)

    first, latter = [], []
    cut = width // 2
    for n in range(2):
        columns = slice(n * cut, (n + 1) * cut)
        if n:
            attended = after(attended, first[-1])
        projected = jnp.dot(attended, weight[:, columns], preferred_element_type=jnp.float32)
        first.append((residual_in[:, columns].astype(jnp.float32) + projected).astype(jnp.bfloat16))
        handed = lax.ppermute(first[-1], "segment", [(0, 1)])
        latter.append((handed.astype(jnp.float32) + projected).astype(jnp.bfloat16))
    first, latter = jnp.concatenate(first, axis=1), jnp.concatenate(latter, axis=1)
    return jnp.where(lax.axis_index("segment") == 0, first, latter)[None]


def solution(mesh):
    fine = Mesh(mesh.devices.reshape(2, NZ, NX, NY), ("segment",) + SEQ)
    in_specs = (
        P(SEQ, None),
        P("segment", SEQ, None),
        P("segment", SEQ, None),
        P("segment", SEQ, None),
        P("segment", None),
        P("segment", None),
        P("segment", SEQ, None, None),
        P(),
        P("segment", SEQ, None),
    )
    return jax.shard_map(
        per_device, mesh=fine, in_specs=in_specs, out_specs=P("segment", SEQ, None), check_vma=False
    )
```

```python
import jax
import jax.numpy as jnp
from jax import lax
from jax.experimental import pallas as pl
from jax.experimental.pallas import tpu as pltpu
from jax.sharding import Mesh, PartitionSpec as P

NZ, NX, NY = 8, 4, 4
PLANE = NX * NY
SEQ = ("z", "x", "y")
CHUNKS = ((0,), (-1, 1), (-2, 2), (-3, 3), (4,))
ORDER = sum(CHUNKS, ())
LIGHT = pl.CostEstimate(flops=1, bytes_accessed=1, transcendentals=0)
HEAVY = pl.CostEstimate(flops=50_000_000_000, bytes_accessed=150_000_000, transcendentals=0)


def pack_kernel(slots, half, extra, sel_ref, *refs):
    sources, out_ref, sem = refs[:-2], refs[-2], refs[-1]
    if extra:
        sources, extra_ref = sources[:-1], sources[-1]
    shards = 1 if half else len(sources)
    per_place = shards * slots + extra

    def copy(source, i):
        pltpu.make_async_copy(source, out_ref.at[i], sem).start()

    @pl.loop(0, PLANE)
    def _(p):
        for n in range(shards):
            for s in range(slots):
                i = p * per_place + n * slots + s
                idx = sel_ref[(p * shards + n) * slots + s]
                if half:

                    @pl.when(idx < half)
                    def _(idx=idx, i=i):
                        copy(sources[0].at[idx], i)

                    @pl.when(idx >= half)
                    def _(idx=idx, i=i):
                        copy(sources[1].at[idx - half], i)
                else:
                    copy(sources[n].at[idx], i)
        if extra:
            copy(extra_ref, p * per_place + per_place - 1)

    pltpu.make_async_copy(out_ref, out_ref, sem).wait()


def pack(sel, sources, half=0, extra=None):
    slots = sel.shape[-1]
    block = sources[0].shape[1:]
    extras = [] if extra is None else [extra]
    total = sel.size + PLANE * len(extras)
    return pl.pallas_call(
        lambda *refs: pack_kernel(slots, half, len(extras), *refs),
        out_shape=jax.ShapeDtypeStruct((total,) + block, sources[0].dtype),
        in_specs=[pl.BlockSpec(memory_space=pltpu.SMEM)]
        + [pl.BlockSpec(memory_space=pltpu.VMEM)] * (len(sources) + len(extras)),
        out_specs=pl.BlockSpec(memory_space=pl.ANY),
        scratch_shapes=[pltpu.SemaphoreType.DMA],
        compiler_params=pltpu.CompilerParams(vmem_limit_bytes=24 * 1024 * 1024),
        cost_estimate=HEAVY,
        name="pack_blocks",
    )(sel.reshape(sel.size), *sources, *extras)


LOG2E = 1.4426950408889634


def local_kernel(scale, offset_ref, slope_ref, q_ref, k_ref, v_ref, out_ref):
    h = pl.program_id(0)
    raw = lax.dot_general(
        q_ref[...], k_ref[...], (((1,), (1,)), ((), ())), preferred_element_type=jnp.float32
    )
    rows = lax.broadcasted_iota(jnp.int32, raw.shape, 0)
    cols = lax.broadcasted_iota(jnp.int32, raw.shape, 1)
    distance = jnp.abs(rows - cols).astype(jnp.float32)
    power = raw * (-scale * LOG2E) + (distance * slope_ref[h] - offset_ref[h])
    w = (1.0 / (1.0 + jnp.exp2(power))).astype(jnp.bfloat16)
    out_ref[...] = jnp.dot(w, v_ref[...], preferred_element_type=jnp.float32)


def local_part(offsets, slopes, q, k, v, heads):
    tokens, width = q.shape
    head_size = width // heads
    column = pl.BlockSpec((tokens, head_size), lambda h: (0, h))
    smem = pl.BlockSpec(memory_space=pltpu.SMEM)
    return pl.pallas_call(
        lambda *refs: local_kernel(head_size ** (-0.5), *refs),
        grid=(heads,),
        out_shape=jax.ShapeDtypeStruct((tokens, width), jnp.float32),
        in_specs=[smem] * 2 + [column] * 3,
        out_specs=column,
        cost_estimate=LIGHT,
        name="local_part",
    )(offsets, slopes, q, k, v)


GROUP = 8


def listed_kernel(
    scale, heads, listed, order_ref, bound_ref, slot_ref, near_ref, far_ref, q_ref, got_ref,
    acc_ref, out_ref, total
):
    blk, head_size = got_ref.shape[2:]
    items = order_ref.shape[0]
    begin, end = bound_ref[0], bound_ref[1]
    total[...] = acc_ref[...]

    @pl.loop(0, (end - begin + GROUP - 1) // GROUP)
    def _(group):
        rows = lax.broadcasted_iota(jnp.int32, (blk, blk), 0)
        cols = lax.broadcasted_iota(jnp.int32, (blk, blk), 1)
        apart = (rows - cols).astype(jnp.float32)
        parts = []
        for n in range(GROUP):
            at_order = begin + group * GROUP + n
            i = order_ref[jnp.minimum(at_order, items - 1)]
            slot = jnp.minimum(slot_ref[i], got_ref.shape[0] - 1)
            row, head = i // (heads * listed), lax.rem(i // listed, heads)
            at = (
                pl.ds(pl.multiple_of(row * blk, blk), blk),
                pl.ds(pl.multiple_of(head * head_size, head_size), head_size),
            )
            raw = lax.dot_general(
                q_ref[at], got_ref[slot, 0], (((1,), (1,)), ((), ())),
                preferred_element_type=jnp.float32,
            )
            power = raw * (-scale * LOG2E) + (apart * far_ref[i] + near_ref[i])
            w = (1.0 / (1.0 + jnp.exp2(power))).astype(jnp.bfloat16)
            part = jnp.dot(w, got_ref[slot, 1], preferred_element_type=jnp.float32)
            parts.append((at_order, at, part))
        for at_order, at, part in parts:

            @pl.when(at_order < end)
            def _(at=at, part=part):
                total[at] += part

    out_ref[...] = total[...].astype(out_ref.dtype)


def listed_part(order, bounds, slot, near, far, q, got, acc, heads, listed, dtype):
    tokens, width = q.shape
    smem = pl.BlockSpec(memory_space=pltpu.SMEM)
    vmem = pl.BlockSpec(memory_space=pltpu.VMEM)
    return pl.pallas_call(
        lambda *refs: listed_kernel((width // heads) ** (-0.5), heads, listed, *refs),
        out_shape=jax.ShapeDtypeStruct((tokens, width), dtype),
        in_specs=[smem] * 5 + [vmem] * 3,
        out_specs=vmem,
        scratch_shapes=[pltpu.VMEM((tokens, width), jnp.float32)],
        compiler_params=pltpu.CompilerParams(vmem_limit_bytes=32 * 1024 * 1024),
        cost_estimate=LIGHT,
        name="listed_part",
    )(order, bounds, slot, near, far, q, got, acc)


def after(x, *others):
    return lax.optimization_barrier((x, others))[0]


def per_device(
    residual_in, queries, keys, values, head_offset, head_slope, key_lists, shard_span, out_weight
):
    q, k, v = queries[0], keys[0], values[0]
    offsets, slopes, entries = head_offset[0], head_slope[0], key_lists[0]
    per_shard, heads, listed = entries.shape
    tokens, width = q.shape
    head_size = width // heads
    blk = tokens // per_shard
    rows = per_shard * heads
    items = rows * listed
    slots = 2
    my_z = lax.axis_index("z")
    my_p = lax.axis_index("x") * NY + lax.axis_index("y")

    def blocked(a):
        return a.reshape(per_shard, blk, heads, head_size).transpose(0, 2, 1, 3)

    kv = jnp.stack([blocked(k), blocked(v)], axis=2).reshape(rows, 2, blk, head_size)

    mine = after(entries, kv).reshape(items)
    item_ids = jnp.arange(items, dtype=jnp.int32)
    owner = mine // per_shard
    earlier = item_ids[:, None] > item_ids[None, :]
    rank = jnp.sum((earlier & (owner[:, None] == owner[None, :])).astype(jnp.int32), axis=-1)
    zs = (my_z + jnp.array(ORDER, jnp.int32)) % NZ
    slot_ids = jnp.arange(slots, dtype=jnp.int32)
    here = (
        (owner // PLANE == zs[None, :, None, None])
        & (owner % PLANE == jnp.arange(PLANE, dtype=jnp.int32)[:, None, None, None])
        & (rank == slot_ids[None, None, :, None])
    )
    block_ids = mine % per_shard * heads + item_ids // listed % heads
    wanted = jnp.sum(jnp.where(here, block_ids, 0), axis=-1)
    selected = lax.all_to_all(wanted, ("x", "y"), split_axis=0, concat_axis=0, tiled=True)

    own_span = shard_span[my_z * PLANE + my_p]
    query_at = own_span * tokens + item_ids // (heads * listed) * blk
    key_at = shard_span[owner] * tokens + mine % per_shard * blk
    base = (query_at - key_at).astype(jnp.float32)
    slope = slopes * (LOG2E / (tokens * NZ * PLANE))
    offset = offsets * LOG2E
    def by_item(a):
        return jnp.broadcast_to(a[None, :, None], (per_shard, heads, listed)).reshape(items)

    far_item = jnp.where(base > 0, 1.0, -1.0) * by_item(slope)
    near_item = far_item * base - by_item(offset)
    dz = (owner // PLANE - my_z) % NZ
    chunk = jnp.minimum(dz, NZ - dz)
    pair = (chunk > 0) & (chunk < len(CHUNKS) - 1)
    shard = jnp.where(pair, owner % PLANE * 2 + (dz < NZ // 2), owner % PLANE)
    slot = shard * jnp.where(chunk == 0, slots + 1, slots) + rank
    ahead = (chunk[:, None] < chunk[None, :]) | (
        (chunk[:, None] == chunk[None, :]) & (item_ids[:, None] < item_ids[None, :])
    )
    turn = jnp.sum(ahead.astype(jnp.int32), axis=0)
    order = jnp.sum(jnp.where(turn[:, None] == item_ids[None, :], item_ids[:, None], 0), axis=0)
    edges = jnp.arange(len(CHUNKS) + 1, dtype=jnp.int32)
    edges = jnp.sum((chunk[None, :] < edges[:, None]).astype(jnp.int32), axis=1)

    def part_of(table, n):
        first = sum(len(chunk) for chunk in CHUNKS[:n])
        return table[:, first:first + len(CHUNKS[n])]

    up = [(i, (i + 1) % NZ) for i in range(NZ)]
    down = [(i, (i - 1) % NZ) for i in range(NZ)]
    half = rows // 2

    def served(sent):
        return lax.all_to_all(sent, ("x", "y"), split_axis=0, concat_axis=0, tiled=True)

    def chosen(n, *sources, cut=0, extra=None):
        return pack(part_of(selected, n), sources, cut, extra)

    def added(n, got, acc, dtype=jnp.float32):
        bounds = edges[n:n + 2]
        return listed_part(
            order, bounds, slot, near_item, far_item, q, got, acc, heads, listed, dtype
        )

    def step(pair):
        return lax.ppermute(pair[0], "z", up), lax.ppermute(pair[1], "z", down)

    ring = step((kv, kv))
    packed = chosen(0, kv, extra=out_weight.reshape(kv.shape[1:]))
    got = served(packed)
    acc = local_part(offset, slope, after(q, packed), k, v, heads)
    ring = after(ring, packed, acc)
    for n in (1, 2, 3):
        later = step(ring) if n < 3 else step((ring[0][:half], ring[1][half:]))
        packed = chosen(n, *ring)
        if n > 1:
            acc = added(n - 2, before, after(acc, packed))
        else:
            weight = got.reshape((PLANE, slots + 1) + kv.shape[1:])[:, slots]
            weight = weight.reshape(-1, width)
        if n == 3:
            later = after(later, acc)
            packed = after(packed, later)
        before, sent = got, after(packed, got)
        got = served(sent)
        ring = after(later, sent, acc)
    weight = lax.all_gather(after(weight, ring), "z", axis=0, tiled=True)
    packed = chosen(4, *ring, cut=half)
    acc = added(2, before, after(acc, packed))
    sent = after(packed, got, acc)
    acc = added(3, got, after(acc, sent))
    attended = added(4, served(sent), acc, jnp.bfloat16)

    first, latter = [], []
    cut = width // 2
    for n in range(2):
        columns = slice(n * cut, (n + 1) * cut)
        if n:
            attended = after(attended, first[-1])
        projected = jnp.dot(attended, weight[:, columns], preferred_element_type=jnp.float32)
        first.append((residual_in[:, columns].astype(jnp.float32) + projected).astype(jnp.bfloat16))
        handed = lax.ppermute(first[-1], "segment", [(0, 1)])
        latter.append((handed.astype(jnp.float32) + projected).astype(jnp.bfloat16))
    first, latter = jnp.concatenate(first, axis=1), jnp.concatenate(latter, axis=1)
    return jnp.where(lax.axis_index("segment") == 0, first, latter)[None]


def solution(mesh):
    fine = Mesh(mesh.devices.reshape(2, NZ, NX, NY), ("segment",) + SEQ)
    in_specs = (
        P(SEQ, None),
        P("segment", SEQ, None),
        P("segment", SEQ, None),
        P("segment", SEQ, None),
        P("segment", None),
        P("segment", None),
        P("segment", SEQ, None, None),
        P(),
        P("segment", SEQ, None),
    )
    return jax.shard_map(
        per_device, mesh=fine, in_specs=in_specs, out_specs=P("segment", SEQ, None), check_vma=False
    )
```

```python
import functools

import jax
import jax.numpy as jnp
from jax import lax
from jax.experimental import pallas as pl
from jax.experimental.pallas import tpu as pltpu
from jax.sharding import Mesh, PartitionSpec as P

NZ, NX, NY = 8, 4, 4
PLANE = NX * NY
SEQ = ("z", "x", "y")
CHUNKS = ((0,), (-1, 1), (-2, 2), (-3, 3), (4,))
ORDER = sum(CHUNKS, ())
LIGHT = pl.CostEstimate(flops=1, bytes_accessed=1, transcendentals=0)
LONG = pl.CostEstimate(flops=100_000_000_000, bytes_accessed=150_000_000, transcendentals=0)
HEAVY = pl.CostEstimate(flops=50_000_000_000, bytes_accessed=150_000_000, transcendentals=0)


def pack_kernel(slots, half, extra, sel_ref, *refs):
    sources, out_ref, sem = refs[:-2], refs[-2], refs[-1]
    if extra:
        sources, extra_ref = sources[:-1], sources[-1]
    shards = 1 if half else len(sources)
    per_place = shards * slots + extra

    def copy(source, i):
        pltpu.make_async_copy(source, out_ref.at[i], sem).start()

    @pl.loop(0, PLANE)
    def _(p):
        for n in range(shards):
            for s in range(slots):
                i = p * per_place + n * slots + s
                idx = sel_ref[(p * shards + n) * slots + s]
                if half:

                    @pl.when(idx < half)
                    def _(idx=idx, i=i):
                        copy(sources[0].at[idx], i)

                    @pl.when(idx >= half)
                    def _(idx=idx, i=i):
                        copy(sources[1].at[idx - half], i)
                else:
                    copy(sources[n].at[idx], i)
        if extra:
            copy(extra_ref, p * per_place + per_place - 1)

    pltpu.make_async_copy(out_ref, out_ref, sem).wait()


def pack(sel, sources, half=0, extra=None):
    slots = sel.shape[-1]
    block = sources[0].shape[1:]
    extras = [] if extra is None else [extra]
    total = sel.size + PLANE * len(extras)
    return pl.pallas_call(
        lambda *refs: pack_kernel(slots, half, len(extras), *refs),
        out_shape=jax.ShapeDtypeStruct((total,) + block, sources[0].dtype),
        in_specs=[pl.BlockSpec(memory_space=pltpu.SMEM)]
        + [pl.BlockSpec(memory_space=pltpu.VMEM)] * (len(sources) + len(extras)),
        out_specs=pl.BlockSpec(memory_space=pl.ANY),
        scratch_shapes=[pltpu.SemaphoreType.DMA],
        compiler_params=pltpu.CompilerParams(vmem_limit_bytes=24 * 1024 * 1024),
        cost_estimate=HEAVY,
        name="pack_blocks",
    )(sel.reshape(sel.size), *sources, *extras)


LOG2E = 1.4426950408889634


def local_kernel(scale, offset_ref, slope_ref, q_ref, k_ref, v_ref, out_ref):
    h = pl.program_id(0)
    raw = lax.dot_general(
        q_ref[...], k_ref[...], (((1,), (1,)), ((), ())), preferred_element_type=jnp.float32
    )
    rows = lax.broadcasted_iota(jnp.int32, raw.shape, 0)
    cols = lax.broadcasted_iota(jnp.int32, raw.shape, 1)
    distance = jnp.abs(rows - cols).astype(jnp.float32)
    power = raw * (-scale * LOG2E) + (distance * slope_ref[h] - offset_ref[h])
    w = (1.0 / (1.0 + jnp.exp2(power))).astype(jnp.bfloat16)
    out_ref[...] = jnp.dot(w, v_ref[...], preferred_element_type=jnp.float32)


def local_part(offsets, slopes, q, k, v, heads):
    tokens, width = q.shape
    head_size = width // heads
    column = pl.BlockSpec((tokens, head_size), lambda h: (0, h))
    smem = pl.BlockSpec(memory_space=pltpu.SMEM)
    return pl.pallas_call(
        lambda *refs: local_kernel(head_size ** (-0.5), *refs),
        grid=(heads,),
        out_shape=jax.ShapeDtypeStruct((tokens, width), jnp.float32),
        in_specs=[smem] * 2 + [column] * 3,
        out_specs=column,
        cost_estimate=LIGHT,
        name="local_part",
    )(offsets, slopes, q, k, v)


GROUP = 4
PARTS = 8
TILE = 256


def add_listed(
    scale, heads, listed, order_ref, bound_ref, slot_ref, near_ref, far_ref, q_ref, got_ref, total
):
    blk, head_size = got_ref.shape[2:]
    items = order_ref.shape[0]
    begin, end = bound_ref[0], bound_ref[1]

    @pl.loop(0, (end - begin + GROUP - 1) // GROUP)
    def _(group):
        rows = lax.broadcasted_iota(jnp.int32, (blk, blk), 0)
        cols = lax.broadcasted_iota(jnp.int32, (blk, blk), 1)
        apart = (rows - cols).astype(jnp.float32)
        parts = []
        for n in range(GROUP):
            at_order = begin + group * GROUP + n
            i = order_ref[jnp.minimum(at_order, items - 1)]
            slot = jnp.minimum(slot_ref[i], got_ref.shape[0] - 1)
            row, head = i // (heads * listed), lax.rem(i // listed, heads)
            at = (
                pl.ds(pl.multiple_of(row * blk, blk), blk),
                pl.ds(pl.multiple_of(head * head_size, head_size), head_size),
            )
            raw = lax.dot_general(
                q_ref[at], got_ref[slot, 0], (((1,), (1,)), ((), ())),
                preferred_element_type=jnp.float32,
            )
            power = raw * (-scale * LOG2E) + (apart * far_ref[i] + near_ref[i])
            w = (1.0 / (1.0 + jnp.exp2(power))).astype(jnp.bfloat16)
            part = jnp.dot(w, got_ref[slot, 1], preferred_element_type=jnp.float32)
            parts.append((at_order, at, part))
        for at_order, at, part in parts:

            @pl.when(at_order < end)
            def _(at=at, part=part):
                total[at] += part


def listed_kernel(sizes, *refs):
    acc_ref, out_ref, total = refs[-3:]
    total[...] = acc_ref[...]
    add_listed(*sizes, *refs[:-3], total)
    out_ref[...] = total[...]


def listed_part(order, bounds, slot, near, far, q, got, acc, heads, listed, hint):
    tokens, width = q.shape
    smem = pl.BlockSpec(memory_space=pltpu.SMEM)
    vmem = pl.BlockSpec(memory_space=pltpu.VMEM)
    return pl.pallas_call(
        lambda *refs: listed_kernel(((width // heads) ** (-0.5), heads, listed), *refs),
        out_shape=jax.ShapeDtypeStruct((tokens, width), jnp.float32),
        in_specs=[smem] * 5 + [vmem] * 3,
        out_specs=vmem,
        scratch_shapes=[pltpu.VMEM((tokens, width), jnp.float32)],
        compiler_params=pltpu.CompilerParams(vmem_limit_bytes=60 * 1024 * 1024),
        cost_estimate=hint,
        name="listed_part",
    )(order, bounds, slot, near, far, q, got, acc)


def weight_copies(weight_ref, held, sems, skip):
    rows = held.shape[0] // PARTS
    return [
        pltpu.make_async_copy(
            weight_ref.at[n * rows:(n + 1) * rows, skip:skip + held.shape[1]],
            held.at[n * rows:(n + 1) * rows, :],
            sems.at[n],
        )
        for n in range(PARTS)
    ]


def project_columns(skip, copies, segment_ref, attended_ref, residual_ref, base_ref, first_ref, held):
    for copy in copies:
        copy.wait()
    for n in range(0, held.shape[1], TILE):
        base = jnp.dot(attended_ref[...], held[:, n:n + TILE], preferred_element_type=jnp.float32)
        residual = residual_ref[:, skip + n:skip + n + TILE].astype(jnp.float32)
        base = base + jnp.where(segment_ref[0] == 0, residual, 0.0)
        base_ref[:, n:n + TILE] = base
        first_ref[:, n:n + TILE] = base.astype(first_ref.dtype)


def last_kernel(skip, sizes, *refs):
    acc_ref, segment_ref, weight_ref, residual_ref = refs[7:11]
    attended_ref, base_ref, first_ref, total, held, sems = refs[11:]
    copies = weight_copies(weight_ref, held, sems, skip)
    for copy in copies:
        copy.start()
    total[...] = acc_ref[...]
    add_listed(*sizes, *refs[:7], total)
    attended_ref[...] = total[...].astype(attended_ref.dtype)
    project_columns(
        skip, copies, segment_ref, attended_ref, residual_ref, base_ref, first_ref, held
    )


def next_kernel(skip, attended_ref, segment_ref, weight_ref, residual_ref, base_ref, first_ref, held, sems):
    copies = weight_copies(weight_ref, held, sems, skip)
    for copy in copies:
        copy.start()
    project_columns(
        skip, copies, segment_ref, attended_ref, residual_ref, base_ref, first_ref, held
    )


def project(part, cut, segment, weight, residual, attended=None, pieces=None, sizes=None):
    tokens, width = residual.shape
    skip = part * cut
    smem = pl.BlockSpec(memory_space=pltpu.SMEM)
    vmem = pl.BlockSpec(memory_space=pltpu.VMEM)
    out_shape = [
        jax.ShapeDtypeStruct((tokens, cut), jnp.float32),
        jax.ShapeDtypeStruct((tokens, cut), residual.dtype),
    ]
    scratch = [
        pltpu.VMEM((width, cut), weight.dtype),
        pltpu.SemaphoreType.DMA((PARTS,)),
    ]
    if pieces is None:
        kernel, operands, in_specs = functools.partial(next_kernel, skip), (attended,), [vmem]
    else:
        kernel, operands = functools.partial(last_kernel, skip, sizes), pieces
        in_specs = [smem] * 5 + [vmem] * 3
        scratch.insert(0, pltpu.VMEM((tokens, width), jnp.float32))
        out_shape.insert(0, jax.ShapeDtypeStruct((tokens, width), residual.dtype))
    return pl.pallas_call(
        kernel,
        out_shape=out_shape,
        in_specs=in_specs + [smem, pl.BlockSpec(memory_space=pl.ANY), vmem],
        out_specs=[vmem] * len(out_shape),
        scratch_shapes=scratch,
        compiler_params=pltpu.CompilerParams(vmem_limit_bytes=60 * 1024 * 1024),
        cost_estimate=LONG if pieces else LIGHT,
        name="project",
    )(*operands, segment, weight, residual)


def after(x, *others):
    return lax.optimization_barrier((x, others))[0]


def per_device(
    residual_in, queries, keys, values, head_offset, head_slope, key_lists, shard_span, out_weight
):
    q, k, v = queries[0], keys[0], values[0]
    offsets, slopes, entries = head_offset[0], head_slope[0], key_lists[0]
    per_shard, heads, listed = entries.shape
    tokens, width = q.shape
    head_size = width // heads
    blk = tokens // per_shard
    rows = per_shard * heads
    items = rows * listed
    slots = 2
    my_z = lax.axis_index("z")
    my_p = lax.axis_index("x") * NY + lax.axis_index("y")

    def blocked(a):
        return a.reshape(per_shard, blk, heads, head_size).transpose(0, 2, 1, 3)

    kv = jnp.stack([blocked(k), blocked(v)], axis=2).reshape(rows, 2, blk, head_size)

    mine = after(entries, kv).reshape(items)
    item_ids = jnp.arange(items, dtype=jnp.int32)
    owner = mine // per_shard
    earlier = item_ids[:, None] > item_ids[None, :]
    rank = jnp.sum((earlier & (owner[:, None] == owner[None, :])).astype(jnp.int32), axis=-1)
    zs = (my_z + jnp.array(ORDER, jnp.int32)) % NZ
    slot_ids = jnp.arange(slots, dtype=jnp.int32)
    here = (
        (owner // PLANE == zs[None, :, None, None])
        & (owner % PLANE == jnp.arange(PLANE, dtype=jnp.int32)[:, None, None, None])
        & (rank == slot_ids[None, None, :, None])
    )
    block_ids = mine % per_shard * heads + item_ids // listed % heads
    wanted = jnp.sum(jnp.where(here, block_ids, 0), axis=-1)
    selected = lax.all_to_all(wanted, ("x", "y"), split_axis=0, concat_axis=0, tiled=True)

    own_span = shard_span[my_z * PLANE + my_p]
    query_at = own_span * tokens + item_ids // (heads * listed) * blk
    key_at = shard_span[owner] * tokens + mine % per_shard * blk
    base = (query_at - key_at).astype(jnp.float32)
    slope = slopes * (LOG2E / (tokens * NZ * PLANE))
    offset = offsets * LOG2E
    def by_item(a):
        return jnp.broadcast_to(a[None, :, None], (per_shard, heads, listed)).reshape(items)

    far_item = jnp.where(base > 0, 1.0, -1.0) * by_item(slope)
    near_item = far_item * base - by_item(offset)
    dz = (owner // PLANE - my_z) % NZ
    chunk = jnp.minimum(dz, NZ - dz)
    pair = (chunk > 0) & (chunk < len(CHUNKS) - 1)
    shard = jnp.where(pair, owner % PLANE * 2 + (dz < NZ // 2), owner % PLANE)
    slot = shard * jnp.where(chunk == 0, slots + 1, slots) + rank
    ahead = (chunk[:, None] < chunk[None, :]) | (
        (chunk[:, None] == chunk[None, :]) & (item_ids[:, None] < item_ids[None, :])
    )
    turn = jnp.sum(ahead.astype(jnp.int32), axis=0)
    order = jnp.sum(jnp.where(turn[:, None] == item_ids[None, :], item_ids[:, None], 0), axis=0)
    edges = jnp.arange(len(CHUNKS) + 1, dtype=jnp.int32)
    edges = jnp.sum((chunk[None, :] < edges[:, None]).astype(jnp.int32), axis=1)

    def part_of(table, n):
        first = sum(len(chunk) for chunk in CHUNKS[:n])
        return table[:, first:first + len(CHUNKS[n])]

    up = [(i, (i + 1) % NZ) for i in range(NZ)]
    down = [(i, (i - 1) % NZ) for i in range(NZ)]
    half = rows // 2

    def served(sent):
        return lax.all_to_all(sent, ("x", "y"), split_axis=0, concat_axis=0, tiled=True)

    def chosen(n, *sources, cut=0, extra=None):
        return pack(part_of(selected, n), sources, cut, extra)

    def added(n, got, acc):
        bounds = edges[n:n + 2]
        return listed_part(
            order, bounds, slot, near_item, far_item, q, got, acc, heads, listed,
            LONG if n > 2 else LIGHT,
        )

    def step(pair):
        return lax.ppermute(pair[0], "z", up), lax.ppermute(pair[1], "z", down)

    ring = step((kv, kv))
    packed = chosen(0, kv, extra=out_weight.reshape(kv.shape[1:]))
    got = served(packed)
    acc = local_part(offset, slope, after(q, packed), k, v, heads)
    ring = after(ring, packed, acc)
    for n in (1, 2, 3):
        later = step(ring) if n < 3 else step((ring[0][:half], ring[1][half:]))
        packed = chosen(n, *ring)
        if n > 1:
            acc = added(n - 2, before, after(acc, packed))
        else:
            weight = got.reshape((PLANE, slots + 1) + kv.shape[1:])[:, slots]
            weight = weight.reshape(-1, width)
        if n == 3:
            weight = lax.all_gather(after(weight, ring), "z", axis=0, tiled=True)
        before, sent = got, after(packed, got)
        got = served(sent)
        ring = after(later, sent, acc)
    packed = chosen(4, *ring, cut=half)
    acc = added(2, before, after(acc, packed))
    sent = after(packed, got, acc)
    acc = added(3, got, after(acc, sent))
    last = served(sent)

    cut = width // 2
    segment = lax.axis_index("segment").reshape(1)
    pieces = (order, edges[4:6], slot, near_item, far_item, q, last, acc)
    sizes = (head_size ** (-0.5), heads, listed)
    attended, left, sent = project(
        0, cut, segment, weight, residual_in, pieces=pieces, sizes=sizes
    )
    left_handed = lax.ppermute(sent, "segment", [(0, 1)])
    attended = after(attended, sent)
    right = jnp.dot(attended, weight[:, cut:], preferred_element_type=jnp.float32)
    residual = residual_in[:, cut:].astype(jnp.float32)
    right = right + jnp.where(segment == 0, residual, 0.0)
    right_handed = lax.ppermute(right.astype(jnp.bfloat16), "segment", [(0, 1)])
    handed = ((left_handed, left), (right_handed, right))
    out = [(part.astype(jnp.float32) + rest).astype(jnp.bfloat16) for part, rest in handed]
    return jnp.concatenate(out, axis=1)[None]


def solution(mesh):
    fine = Mesh(mesh.devices.reshape(2, NZ, NX, NY), ("segment",) + SEQ)
    in_specs = (
        P(SEQ, None),
        P("segment", SEQ, None),
        P("segment", SEQ, None),
        P("segment", SEQ, None),
        P("segment", None),
        P("segment", None),
        P("segment", SEQ, None, None),
        P(),
        P("segment", SEQ, None),
    )
    return jax.shard_map(
        per_device, mesh=fine, in_specs=in_specs, out_specs=P("segment", SEQ, None), check_vma=False
    )
```

```python
import functools

import jax
import jax.numpy as jnp
from jax import lax
from jax.experimental import pallas as pl
from jax.experimental.pallas import tpu as pltpu
from jax.sharding import Mesh, PartitionSpec as P

NZ, NX, NY = 8, 4, 4
PLANE = NX * NY
SEQ = ("z", "x", "y")
CHUNKS = ((0,), (-1, 1), (-2, 2), (-3, 3), (4,))
ORDER = sum(CHUNKS, ())
LIGHT = pl.CostEstimate(flops=1, bytes_accessed=1, transcendentals=0)
LONG = pl.CostEstimate(flops=100_000_000_000, bytes_accessed=150_000_000, transcendentals=0)
HEAVY = pl.CostEstimate(flops=50_000_000_000, bytes_accessed=150_000_000, transcendentals=0)


def pack_kernel(slots, half, extra, sel_ref, *refs):
    sources, out_ref, sem = refs[:-2], refs[-2], refs[-1]
    if extra:
        sources, extra_ref = sources[:-1], sources[-1]
    shards = 1 if half else len(sources)
    per_place = shards * slots + extra

    def copy(source, i):
        pltpu.make_async_copy(source, out_ref.at[i], sem).start()

    @pl.loop(0, PLANE)
    def _(p):
        for n in range(shards):
            for s in range(slots):
                i = p * per_place + n * slots + s
                idx = sel_ref[(p * shards + n) * slots + s]
                if half:

                    @pl.when(idx < half)
                    def _(idx=idx, i=i):
                        copy(sources[0].at[idx], i)

                    @pl.when(idx >= half)
                    def _(idx=idx, i=i):
                        copy(sources[1].at[idx - half], i)
                else:
                    copy(sources[n].at[idx], i)
        if extra:
            copy(extra_ref, p * per_place + per_place - 1)

    pltpu.make_async_copy(out_ref, out_ref, sem).wait()


def pack(sel, sources, half=0, extra=None):
    slots = sel.shape[-1]
    block = sources[0].shape[1:]
    extras = [] if extra is None else [extra]
    total = sel.size + PLANE * len(extras)
    return pl.pallas_call(
        lambda *refs: pack_kernel(slots, half, len(extras), *refs),
        out_shape=jax.ShapeDtypeStruct((total,) + block, sources[0].dtype),
        in_specs=[pl.BlockSpec(memory_space=pltpu.SMEM)]
        + [pl.BlockSpec(memory_space=pltpu.VMEM)] * (len(sources) + len(extras)),
        out_specs=pl.BlockSpec(memory_space=pl.ANY),
        scratch_shapes=[pltpu.SemaphoreType.DMA],
        compiler_params=pltpu.CompilerParams(vmem_limit_bytes=(24 if extras else 60) * 1024 * 1024),
        cost_estimate=HEAVY,
        name="pack_blocks",
    )(sel.reshape(sel.size), *sources, *extras)


LOG2E = 1.4426950408889634


def local_kernel(scale, offset_ref, slope_ref, q_ref, k_ref, v_ref, out_ref):
    h = pl.program_id(0)
    raw = lax.dot_general(
        q_ref[...], k_ref[...], (((1,), (1,)), ((), ())), preferred_element_type=jnp.float32
    )
    rows = lax.broadcasted_iota(jnp.int32, raw.shape, 0)
    cols = lax.broadcasted_iota(jnp.int32, raw.shape, 1)
    distance = jnp.abs(rows - cols).astype(jnp.float32)
    power = raw * (-scale * LOG2E) + (distance * slope_ref[h] - offset_ref[h])
    w = (1.0 / (1.0 + jnp.exp2(power))).astype(jnp.bfloat16)
    out_ref[...] = jnp.dot(w, v_ref[...], preferred_element_type=jnp.float32)


def local_part(offsets, slopes, q, k, v, heads):
    tokens, width = q.shape
    head_size = width // heads
    column = pl.BlockSpec((tokens, head_size), lambda h: (0, h))
    smem = pl.BlockSpec(memory_space=pltpu.SMEM)
    return pl.pallas_call(
        lambda *refs: local_kernel(head_size ** (-0.5), *refs),
        grid=(heads,),
        out_shape=jax.ShapeDtypeStruct((tokens, width), jnp.float32),
        in_specs=[smem] * 2 + [column] * 3,
        out_specs=column,
        cost_estimate=LIGHT,
        name="local_part",
    )(offsets, slopes, q, k, v)


GROUP = 4
PARTS = 8
TILE = 256


def add_listed(
    scale, heads, listed, order_ref, bound_ref, slot_ref, near_ref, far_ref, q_ref, got_ref, total
):
    blk, head_size = got_ref.shape[2:]
    items = order_ref.shape[0]
    begin, end = bound_ref[0], bound_ref[1]

    @pl.loop(0, (end - begin + GROUP - 1) // GROUP)
    def _(group):
        rows = lax.broadcasted_iota(jnp.int32, (blk, blk), 0)
        cols = lax.broadcasted_iota(jnp.int32, (blk, blk), 1)
        apart = (rows - cols).astype(jnp.float32)
        parts = []
        for n in range(GROUP):
            at_order = begin + group * GROUP + n
            i = order_ref[jnp.minimum(at_order, items - 1)]
            slot = jnp.minimum(slot_ref[i], got_ref.shape[0] - 1)
            row, head = i // (heads * listed), lax.rem(i // listed, heads)
            at = (
                pl.ds(pl.multiple_of(row * blk, blk), blk),
                pl.ds(pl.multiple_of(head * head_size, head_size), head_size),
            )
            raw = lax.dot_general(
                q_ref[at], got_ref[slot, 0], (((1,), (1,)), ((), ())),
                preferred_element_type=jnp.float32,
            )
            power = raw * (-scale * LOG2E) + (apart * far_ref[i] + near_ref[i])
            w = (1.0 / (1.0 + jnp.exp2(power))).astype(jnp.bfloat16)
            part = jnp.dot(w, got_ref[slot, 1], preferred_element_type=jnp.float32)
            parts.append((at_order, at, part))
        for at_order, at, part in parts:

            @pl.when(at_order < end)
            def _(at=at, part=part):
                total[at] += part


def listed_kernel(sizes, *refs):
    acc_ref, out_ref, total = refs[-3:]
    total[...] = acc_ref[...]
    add_listed(*sizes, *refs[:-3], total)
    out_ref[...] = total[...]


def listed_part(order, bounds, slot, near, far, q, got, acc, heads, listed, hint):
    tokens, width = q.shape
    smem = pl.BlockSpec(memory_space=pltpu.SMEM)
    vmem = pl.BlockSpec(memory_space=pltpu.VMEM)
    return pl.pallas_call(
        lambda *refs: listed_kernel(((width // heads) ** (-0.5), heads, listed), *refs),
        out_shape=jax.ShapeDtypeStruct((tokens, width), jnp.float32),
        in_specs=[smem] * 5 + [vmem] * 3,
        out_specs=vmem,
        scratch_shapes=[pltpu.VMEM((tokens, width), jnp.float32)],
        compiler_params=pltpu.CompilerParams(vmem_limit_bytes=60 * 1024 * 1024),
        cost_estimate=hint,
        name="listed_part",
    )(order, bounds, slot, near, far, q, got, acc)


def weight_copies(weight_ref, held, sems, skip):
    rows = held.shape[0] // PARTS
    return [
        pltpu.make_async_copy(
            weight_ref.at[n * rows:(n + 1) * rows, skip:skip + held.shape[1]],
            held.at[n * rows:(n + 1) * rows, :],
            sems.at[n],
        )
        for n in range(PARTS)
    ]


def project_columns(skip, copies, segment_ref, attended_ref, residual_ref, base_ref, first_ref, held):
    for copy in copies:
        copy.wait()
    for n in range(0, held.shape[1], TILE):
        base = jnp.dot(attended_ref[...], held[:, n:n + TILE], preferred_element_type=jnp.float32)
        residual = residual_ref[:, skip + n:skip + n + TILE].astype(jnp.float32)
        base = base + jnp.where(segment_ref[0] == 0, residual, 0.0)
        base_ref[:, n:n + TILE] = base
        first_ref[:, n:n + TILE] = base.astype(first_ref.dtype)


def last_kernel(skip, sizes, *refs):
    acc_ref, segment_ref, weight_ref, residual_ref = refs[7:11]
    attended_ref, base_ref, first_ref, total, held, sems = refs[11:]
    copies = weight_copies(weight_ref, held, sems, skip)
    for copy in copies:
        copy.start()
    total[...] = acc_ref[...]
    add_listed(*sizes, *refs[:7], total)
    attended_ref[...] = total[...].astype(attended_ref.dtype)
    project_columns(
        skip, copies, segment_ref, attended_ref, residual_ref, base_ref, first_ref, held
    )


def next_kernel(skip, attended_ref, segment_ref, weight_ref, residual_ref, base_ref, first_ref, held, sems):
    copies = weight_copies(weight_ref, held, sems, skip)
    for copy in copies:
        copy.start()
    project_columns(
        skip, copies, segment_ref, attended_ref, residual_ref, base_ref, first_ref, held
    )


def project(part, cut, segment, weight, residual, attended=None, pieces=None, sizes=None):
    tokens, width = residual.shape
    skip = part * cut
    smem = pl.BlockSpec(memory_space=pltpu.SMEM)
    vmem = pl.BlockSpec(memory_space=pltpu.VMEM)
    out_shape = [
        jax.ShapeDtypeStruct((tokens, cut), jnp.float32),
        jax.ShapeDtypeStruct((tokens, cut), residual.dtype),
    ]
    scratch = [
        pltpu.VMEM((width, cut), weight.dtype),
        pltpu.SemaphoreType.DMA((PARTS,)),
    ]
    if pieces is None:
        kernel, operands, in_specs = functools.partial(next_kernel, skip), (attended,), [vmem]
    else:
        kernel, operands = functools.partial(last_kernel, skip, sizes), pieces
        in_specs = [smem] * 5 + [vmem] * 3
        scratch.insert(0, pltpu.VMEM((tokens, width), jnp.float32))
        out_shape.insert(0, jax.ShapeDtypeStruct((tokens, width), residual.dtype))
    return pl.pallas_call(
        kernel,
        out_shape=out_shape,
        in_specs=in_specs + [smem, pl.BlockSpec(memory_space=pl.ANY), vmem],
        out_specs=[vmem] * len(out_shape),
        scratch_shapes=scratch,
        compiler_params=pltpu.CompilerParams(vmem_limit_bytes=60 * 1024 * 1024),
        cost_estimate=LONG if pieces else LIGHT,
        name="project",
    )(*operands, segment, weight, residual)


def after(x, *others):
    return lax.optimization_barrier((x, others))[0]


def per_device(
    residual_in, queries, keys, values, head_offset, head_slope, key_lists, shard_span, out_weight
):
    q, k, v = queries[0], keys[0], values[0]
    offsets, slopes, entries = head_offset[0], head_slope[0], key_lists[0]
    per_shard, heads, listed = entries.shape
    tokens, width = q.shape
    head_size = width // heads
    blk = tokens // per_shard
    rows = per_shard * heads
    items = rows * listed
    slots = 2
    my_z = lax.axis_index("z")
    my_p = lax.axis_index("x") * NY + lax.axis_index("y")

    def blocked(a):
        return a.reshape(per_shard, blk, heads, head_size).transpose(0, 2, 1, 3)

    kv = jnp.stack([blocked(k), blocked(v)], axis=2).reshape(rows, 2, blk, head_size)

    mine = after(entries, kv).reshape(items)
    item_ids = jnp.arange(items, dtype=jnp.int32)
    owner = mine // per_shard
    earlier = item_ids[:, None] > item_ids[None, :]
    rank = jnp.sum((earlier & (owner[:, None] == owner[None, :])).astype(jnp.int32), axis=-1)
    zs = (my_z + jnp.array(ORDER, jnp.int32)) % NZ
    slot_ids = jnp.arange(slots, dtype=jnp.int32)
    here = (
        (owner // PLANE == zs[None, :, None, None])
        & (owner % PLANE == jnp.arange(PLANE, dtype=jnp.int32)[:, None, None, None])
        & (rank == slot_ids[None, None, :, None])
    )
    block_ids = mine % per_shard * heads + item_ids // listed % heads
    wanted = jnp.sum(jnp.where(here, block_ids, 0), axis=-1)
    selected = lax.all_to_all(wanted, ("x", "y"), split_axis=0, concat_axis=0, tiled=True)

    own_span = shard_span[my_z * PLANE + my_p]
    query_at = own_span * tokens + item_ids // (heads * listed) * blk
    key_at = shard_span[owner] * tokens + mine % per_shard * blk
    base = (query_at - key_at).astype(jnp.float32)
    slope = slopes * (LOG2E / (tokens * NZ * PLANE))
    offset = offsets * LOG2E
    def by_item(a):
        return jnp.broadcast_to(a[None, :, None], (per_shard, heads, listed)).reshape(items)

    far_item = jnp.where(base > 0, 1.0, -1.0) * by_item(slope)
    near_item = far_item * base - by_item(offset)
    dz = (owner // PLANE - my_z) % NZ
    chunk = jnp.minimum(dz, NZ - dz)
    pair = (chunk > 0) & (chunk < len(CHUNKS) - 1)
    shard = jnp.where(pair, owner % PLANE * 2 + (dz < NZ // 2), owner % PLANE)
    slot = shard * jnp.where(chunk == 0, slots + 1, slots) + rank
    ahead = (chunk[:, None] < chunk[None, :]) | (
        (chunk[:, None] == chunk[None, :]) & (item_ids[:, None] < item_ids[None, :])
    )
    turn = jnp.sum(ahead.astype(jnp.int32), axis=0)
    order = jnp.sum(jnp.where(turn[:, None] == item_ids[None, :], item_ids[:, None], 0), axis=0)
    edges = jnp.arange(len(CHUNKS) + 1, dtype=jnp.int32)
    edges = jnp.sum((chunk[None, :] < edges[:, None]).astype(jnp.int32), axis=1)

    def part_of(table, n):
        first = sum(len(chunk) for chunk in CHUNKS[:n])
        return table[:, first:first + len(CHUNKS[n])]

    up = [(i, (i + 1) % NZ) for i in range(NZ)]
    down = [(i, (i - 1) % NZ) for i in range(NZ)]
    half = rows // 2

    def served(sent):
        return lax.all_to_all(sent, ("x", "y"), split_axis=0, concat_axis=0, tiled=True)

    def chosen(n, *sources, cut=0, extra=None):
        return pack(part_of(selected, n), sources, cut, extra)

    def added(n, got, acc):
        bounds = edges[n:n + 2]
        return listed_part(
            order, bounds, slot, near_item, far_item, q, got, acc, heads, listed,
            LONG if n > 2 else LIGHT,
        )

    def step(pair):
        return lax.ppermute(pair[0], "z", up), lax.ppermute(pair[1], "z", down)

    ring = step((kv, kv))
    packed = chosen(0, kv, extra=out_weight.reshape(kv.shape[1:]))
    got = served(packed)
    acc = local_part(offset, slope, after(q, packed), k, v, heads)
    ring = after(ring, packed, acc)
    for n in (1, 2, 3):
        later = step(ring) if n < 3 else step((ring[0][:half], ring[1][half:]))
        packed = chosen(n, *ring)
        if n > 1:
            acc = added(n - 2, before, after(acc, packed))
        else:
            weight = got.reshape((PLANE, slots + 1) + kv.shape[1:])[:, slots]
            weight = weight.reshape(-1, width)
        if n == 3:
            weight = lax.all_gather(after(weight, ring), "z", axis=0, tiled=True)
        before, sent = got, after(packed, got)
        got = served(sent)
        ring = after(later, sent, acc)
    packed = chosen(4, *ring, cut=half)
    acc = added(2, before, after(acc, packed))
    sent = after(packed, got, acc)
    acc = added(3, got, after(acc, sent))
    last = served(sent)

    cut = width * 3 // 4
    segment = lax.axis_index("segment").reshape(1)
    pieces = (order, edges[4:6], slot, near_item, far_item, q, last, acc)
    sizes = (head_size ** (-0.5), heads, listed)
    attended, left, sent = project(
        0, cut, segment, weight, residual_in, pieces=pieces, sizes=sizes
    )
    left_handed = lax.ppermute(sent, "segment", [(0, 1)])
    attended = after(attended, sent)
    right = jnp.dot(attended, weight[:, cut:], preferred_element_type=jnp.float32)
    residual = residual_in[:, cut:].astype(jnp.float32)
    right = right + jnp.where(segment == 0, residual, 0.0)
    right_handed = lax.ppermute(right.astype(jnp.bfloat16), "segment", [(0, 1)])
    handed = ((left_handed, left), (right_handed, right))
    out = [(part.astype(jnp.float32) + rest).astype(jnp.bfloat16) for part, rest in handed]
    return jnp.concatenate(out, axis=1)[None]


def solution(mesh):
    fine = Mesh(mesh.devices.reshape(2, NZ, NX, NY), ("segment",) + SEQ)
    in_specs = (
        P(SEQ, None),
        P("segment", SEQ, None),
        P("segment", SEQ, None),
        P("segment", SEQ, None),
        P("segment", None),
        P("segment", None),
        P("segment", SEQ, None, None),
        P(),
        P("segment", SEQ, None),
    )
    return jax.shard_map(
        per_device, mesh=fine, in_specs=in_specs, out_specs=P("segment", SEQ, None), check_vma=False
    )
```

```python
import functools

import jax
import jax.numpy as jnp
from jax import lax
from jax.experimental import pallas as pl
from jax.experimental.pallas import tpu as pltpu
from jax.sharding import Mesh, PartitionSpec as P

NZ, NX, NY = 8, 4, 4
PLANE = NX * NY
SEQ = ("z", "x", "y")
CHUNKS = ((0,), (-1, 1), (-2, 2), (-3, 3), (4,))
ORDER = sum(CHUNKS, ())
LIGHT = pl.CostEstimate(flops=1, bytes_accessed=1, transcendentals=0)
LONG = pl.CostEstimate(flops=100_000_000_000, bytes_accessed=150_000_000, transcendentals=0)
HEAVY = pl.CostEstimate(flops=50_000_000_000, bytes_accessed=150_000_000, transcendentals=0)


def pack_kernel(slots, half, extra, sel_ref, *refs):
    sources, out_ref, sem = refs[:-2], refs[-2], refs[-1]
    if extra:
        sources, extra_ref = sources[:-1], sources[-1]
    shards = 1 if half else len(sources)
    per_place = shards * slots + extra

    def copy(source, i):
        pltpu.make_async_copy(source, out_ref.at[i], sem).start()

    @pl.loop(0, PLANE)
    def _(p):
        for n in range(shards):
            for s in range(slots):
                i = p * per_place + n * slots + s
                idx = sel_ref[(p * shards + n) * slots + s]
                if half:

                    @pl.when(idx < half)
                    def _(idx=idx, i=i):
                        copy(sources[0].at[idx], i)

                    @pl.when(idx >= half)
                    def _(idx=idx, i=i):
                        copy(sources[1].at[idx - half], i)
                else:
                    copy(sources[n].at[idx], i)
        if extra:
            copy(extra_ref, p * per_place + per_place - 1)

    pltpu.make_async_copy(out_ref, out_ref, sem).wait()


def pack(sel, sources, half=0, extra=None):
    slots = sel.shape[-1]
    block = sources[0].shape[1:]
    extras = [] if extra is None else [extra]
    total = sel.size + PLANE * len(extras)
    return pl.pallas_call(
        lambda *refs: pack_kernel(slots, half, len(extras), *refs),
        out_shape=jax.ShapeDtypeStruct((total,) + block, sources[0].dtype),
        in_specs=[pl.BlockSpec(memory_space=pltpu.SMEM)]
        + [pl.BlockSpec(memory_space=pltpu.VMEM)] * (len(sources) + len(extras)),
        out_specs=pl.BlockSpec(memory_space=pl.ANY),
        scratch_shapes=[pltpu.SemaphoreType.DMA],
        compiler_params=pltpu.CompilerParams(vmem_limit_bytes=(24 if extras else 60) * 1024 * 1024),
        cost_estimate=HEAVY,
        name="pack_blocks",
    )(sel.reshape(sel.size), *sources, *extras)


LOG2E = 1.4426950408889634


def local_kernel(scale, offset_ref, slope_ref, q_ref, k_ref, v_ref, out_ref):
    h = pl.program_id(0)
    raw = lax.dot_general(
        q_ref[...], k_ref[...], (((1,), (1,)), ((), ())), preferred_element_type=jnp.float32
    )
    rows = lax.broadcasted_iota(jnp.int32, raw.shape, 0)
    cols = lax.broadcasted_iota(jnp.int32, raw.shape, 1)
    distance = jnp.abs(rows - cols).astype(jnp.float32)
    power = raw * (-scale * LOG2E) + (distance * slope_ref[h] - offset_ref[h])
    w = (1.0 / (1.0 + jnp.exp2(power))).astype(jnp.bfloat16)
    out_ref[...] = jnp.dot(w, v_ref[...], preferred_element_type=jnp.float32)


def local_part(offsets, slopes, q, k, v, heads):
    tokens, width = q.shape
    head_size = width // heads
    column = pl.BlockSpec((tokens, head_size), lambda h: (0, h))
    smem = pl.BlockSpec(memory_space=pltpu.SMEM)
    return pl.pallas_call(
        lambda *refs: local_kernel(head_size ** (-0.5), *refs),
        grid=(heads,),
        out_shape=jax.ShapeDtypeStruct((tokens, width), jnp.float32),
        in_specs=[smem] * 2 + [column] * 3,
        out_specs=column,
        cost_estimate=LIGHT,
        name="local_part",
    )(offsets, slopes, q, k, v)


GROUP = 4
PARTS = 8
TILE = 256


def add_listed(
    scale, heads, listed, order_ref, bound_ref, slot_ref, near_ref, far_ref, q_ref, got_ref, total
):
    blk, head_size = got_ref.shape[2:]
    items = order_ref.shape[0]
    begin, end = bound_ref[0], bound_ref[1]

    @pl.loop(0, (end - begin + GROUP - 1) // GROUP)
    def _(group):
        rows = lax.broadcasted_iota(jnp.int32, (blk, blk), 0)
        cols = lax.broadcasted_iota(jnp.int32, (blk, blk), 1)
        apart = (rows - cols).astype(jnp.float32)
        parts = []
        for n in range(GROUP):
            at_order = begin + group * GROUP + n
            i = order_ref[jnp.minimum(at_order, items - 1)]
            slot = jnp.minimum(slot_ref[i], got_ref.shape[0] - 1)
            row, head = i // (heads * listed), lax.rem(i // listed, heads)
            at = (
                pl.ds(pl.multiple_of(row * blk, blk), blk),
                pl.ds(pl.multiple_of(head * head_size, head_size), head_size),
            )
            raw = lax.dot_general(
                q_ref[at], got_ref[slot, 0], (((1,), (1,)), ((), ())),
                preferred_element_type=jnp.float32,
            )
            power = raw * (-scale * LOG2E) + (apart * far_ref[i] + near_ref[i])
            w = (1.0 / (1.0 + jnp.exp2(power))).astype(jnp.bfloat16)
            part = jnp.dot(w, got_ref[slot, 1], preferred_element_type=jnp.float32)
            parts.append((at_order, at, part))
        for at_order, at, part in parts:

            @pl.when(at_order < end)
            def _(at=at, part=part):
                total[at] += part


def listed_kernel(sizes, *refs):
    acc_ref, out_ref, total = refs[-3:]
    total[...] = acc_ref[...]
    add_listed(*sizes, *refs[:-3], total)
    out_ref[...] = total[...]


def listed_part(order, bounds, slot, near, far, q, got, acc, heads, listed, hint):
    tokens, width = q.shape
    smem = pl.BlockSpec(memory_space=pltpu.SMEM)
    vmem = pl.BlockSpec(memory_space=pltpu.VMEM)
    return pl.pallas_call(
        lambda *refs: listed_kernel(((width // heads) ** (-0.5), heads, listed), *refs),
        out_shape=jax.ShapeDtypeStruct((tokens, width), jnp.float32),
        in_specs=[smem] * 5 + [vmem] * 3,
        out_specs=vmem,
        scratch_shapes=[pltpu.VMEM((tokens, width), jnp.float32)],
        compiler_params=pltpu.CompilerParams(vmem_limit_bytes=60 * 1024 * 1024),
        cost_estimate=hint,
        name="listed_part",
    )(order, bounds, slot, near, far, q, got, acc)


def weight_copies(weight_ref, held, sems, skip):
    rows = held.shape[0] // PARTS
    return [
        pltpu.make_async_copy(
            weight_ref.at[n * rows:(n + 1) * rows, skip:skip + held.shape[1]],
            held.at[n * rows:(n + 1) * rows, :],
            sems.at[n],
        )
        for n in range(PARTS)
    ]


def project_columns(skip, copies, segment_ref, attended_ref, residual_ref, base_ref, first_ref, held):
    for copy in copies:
        copy.wait()
    for n in range(0, held.shape[1], TILE):
        base = jnp.dot(attended_ref[...], held[:, n:n + TILE], preferred_element_type=jnp.float32)
        residual = residual_ref[:, skip + n:skip + n + TILE].astype(jnp.float32)
        base = base + jnp.where(segment_ref[0] == 0, residual, 0.0)
        base_ref[:, n:n + TILE] = base
        first_ref[:, n:n + TILE] = base.astype(first_ref.dtype)


def last_kernel(skip, sizes, *refs):
    acc_ref, segment_ref, weight_ref, residual_ref = refs[7:11]
    attended_ref, base_ref, first_ref, total, held, sems = refs[11:]
    copies = weight_copies(weight_ref, held, sems, skip)
    for copy in copies:
        copy.start()
    total[...] = acc_ref[...]
    add_listed(*sizes, *refs[:7], total)
    attended_ref[...] = total[...].astype(attended_ref.dtype)
    project_columns(
        skip, copies, segment_ref, attended_ref, residual_ref, base_ref, first_ref, held
    )


def next_kernel(skip, attended_ref, segment_ref, weight_ref, residual_ref, base_ref, first_ref, held, sems):
    copies = weight_copies(weight_ref, held, sems, skip)
    for copy in copies:
        copy.start()
    project_columns(
        skip, copies, segment_ref, attended_ref, residual_ref, base_ref, first_ref, held
    )


def project(part, cut, segment, weight, residual, attended=None, pieces=None, sizes=None):
    tokens, width = residual.shape
    skip = part * cut
    smem = pl.BlockSpec(memory_space=pltpu.SMEM)
    vmem = pl.BlockSpec(memory_space=pltpu.VMEM)
    out_shape = [
        jax.ShapeDtypeStruct((tokens, cut), jnp.float32),
        jax.ShapeDtypeStruct((tokens, cut), residual.dtype),
    ]
    scratch = [
        pltpu.VMEM((width, cut), weight.dtype),
        pltpu.SemaphoreType.DMA((PARTS,)),
    ]
    if pieces is None:
        kernel, operands, in_specs = functools.partial(next_kernel, skip), (attended,), [vmem]
    else:
        kernel, operands = functools.partial(last_kernel, skip, sizes), pieces
        in_specs = [smem] * 5 + [vmem] * 3
        scratch.insert(0, pltpu.VMEM((tokens, width), jnp.float32))
        out_shape.insert(0, jax.ShapeDtypeStruct((tokens, width), residual.dtype))
    return pl.pallas_call(
        kernel,
        out_shape=out_shape,
        in_specs=in_specs + [smem, pl.BlockSpec(memory_space=pl.ANY), vmem],
        out_specs=[vmem] * len(out_shape),
        scratch_shapes=scratch,
        compiler_params=pltpu.CompilerParams(vmem_limit_bytes=63 * 1024 * 1024),
        cost_estimate=LONG if pieces else LIGHT,
        name="project",
    )(*operands, segment, weight, residual)


def after(x, *others):
    return lax.optimization_barrier((x, others))[0]


def per_device(
    residual_in, queries, keys, values, head_offset, head_slope, key_lists, shard_span, out_weight
):
    q, k, v = queries[0], keys[0], values[0]
    offsets, slopes, entries = head_offset[0], head_slope[0], key_lists[0]
    per_shard, heads, listed = entries.shape
    tokens, width = q.shape
    head_size = width // heads
    blk = tokens // per_shard
    rows = per_shard * heads
    items = rows * listed
    slots = 2
    my_z = lax.axis_index("z")
    my_p = lax.axis_index("x") * NY + lax.axis_index("y")

    def blocked(a):
        return a.reshape(per_shard, blk, heads, head_size).transpose(0, 2, 1, 3)

    kv = jnp.stack([blocked(k), blocked(v)], axis=2).reshape(rows, 2, blk, head_size)

    mine = after(entries, kv).reshape(items)
    item_ids = jnp.arange(items, dtype=jnp.int32)
    owner = mine // per_shard
    earlier = item_ids[:, None] > item_ids[None, :]
    rank = jnp.sum((earlier & (owner[:, None] == owner[None, :])).astype(jnp.int32), axis=-1)
    zs = (my_z + jnp.array(ORDER, jnp.int32)) % NZ
    slot_ids = jnp.arange(slots, dtype=jnp.int32)
    here = (
        (owner // PLANE == zs[None, :, None, None])
        & (owner % PLANE == jnp.arange(PLANE, dtype=jnp.int32)[:, None, None, None])
        & (rank == slot_ids[None, None, :, None])
    )
    block_ids = mine % per_shard * heads + item_ids // listed % heads
    wanted = jnp.sum(jnp.where(here, block_ids, 0), axis=-1)
    selected = lax.all_to_all(wanted, ("x", "y"), split_axis=0, concat_axis=0, tiled=True)

    own_span = shard_span[my_z * PLANE + my_p]
    query_at = own_span * tokens + item_ids // (heads * listed) * blk
    key_at = shard_span[owner] * tokens + mine % per_shard * blk
    base = (query_at - key_at).astype(jnp.float32)
    slope = slopes * (LOG2E / (tokens * NZ * PLANE))
    offset = offsets * LOG2E
    def by_item(a):
        return jnp.broadcast_to(a[None, :, None], (per_shard, heads, listed)).reshape(items)

    far_item = jnp.where(base > 0, 1.0, -1.0) * by_item(slope)
    near_item = far_item * base - by_item(offset)
    dz = (owner // PLANE - my_z) % NZ
    chunk = jnp.minimum(dz, NZ - dz)
    pair = (chunk > 0) & (chunk < len(CHUNKS) - 1)
    shard = jnp.where(pair, owner % PLANE * 2 + (dz < NZ // 2), owner % PLANE)
    slot = shard * jnp.where(chunk == 0, slots + 1, slots) + rank
    ahead = (chunk[:, None] < chunk[None, :]) | (
        (chunk[:, None] == chunk[None, :]) & (item_ids[:, None] < item_ids[None, :])
    )
    turn = jnp.sum(ahead.astype(jnp.int32), axis=0)
    order = jnp.sum(jnp.where(turn[:, None] == item_ids[None, :], item_ids[:, None], 0), axis=0)
    edges = jnp.arange(len(CHUNKS) + 1, dtype=jnp.int32)
    edges = jnp.sum((chunk[None, :] < edges[:, None]).astype(jnp.int32), axis=1)

    def part_of(table, n):
        first = sum(len(chunk) for chunk in CHUNKS[:n])
        return table[:, first:first + len(CHUNKS[n])]

    up = [(i, (i + 1) % NZ) for i in range(NZ)]
    down = [(i, (i - 1) % NZ) for i in range(NZ)]
    half = rows // 2

    def served(sent):
        return lax.all_to_all(sent, ("x", "y"), split_axis=0, concat_axis=0, tiled=True)

    def chosen(n, *sources, cut=0, extra=None):
        return pack(part_of(selected, n), sources, cut, extra)

    def added(n, got, acc):
        bounds = edges[n:n + 2]
        return listed_part(
            order, bounds, slot, near_item, far_item, q, got, acc, heads, listed,
            LONG if n > 2 else LIGHT,
        )

    def step(pair):
        return lax.ppermute(pair[0], "z", up), lax.ppermute(pair[1], "z", down)

    ring = step((kv, kv))
    packed = chosen(0, kv, extra=out_weight.reshape(kv.shape[1:]))
    got = served(packed)
    acc = local_part(offset, slope, after(q, packed), k, v, heads)
    ring = after(ring, packed, acc)
    for n in (1, 2, 3):
        later = step(ring) if n < 3 else step((ring[0][:half], ring[1][half:]))
        packed = chosen(n, *ring)
        if n > 1:
            acc = added(n - 2, before, after(acc, packed))
        else:
            weight = got.reshape((PLANE, slots + 1) + kv.shape[1:])[:, slots]
            weight = weight.reshape(-1, width)
        if n == 3:
            weight = lax.all_gather(after(weight, ring), "z", axis=0, tiled=True)
        before, sent = got, after(packed, got)
        got = served(sent)
        ring = after(later, sent, acc)
    packed = chosen(4, *ring, cut=half)
    acc = added(2, before, after(acc, packed))
    sent = after(packed, got, acc)
    acc = added(3, got, after(acc, sent))
    last = served(sent)

    cut = width * 3 // 4
    segment = lax.axis_index("segment").reshape(1)
    pieces = (order, edges[4:6], slot, near_item, far_item, q, last, acc)
    sizes = (head_size ** (-0.5), heads, listed)
    attended, left, sent = project(
        0, cut, segment, weight, residual_in, pieces=pieces, sizes=sizes
    )
    left_handed = lax.ppermute(sent, "segment", [(0, 1)])
    attended = after(attended, sent)
    right = jnp.dot(attended, weight[:, cut:], preferred_element_type=jnp.float32)
    residual = residual_in[:, cut:].astype(jnp.float32)
    right = right + jnp.where(segment == 0, residual, 0.0)
    right_handed = lax.ppermute(right.astype(jnp.bfloat16), "segment", [(0, 1)])
    handed = ((left_handed, left), (right_handed, right))
    out = [(part.astype(jnp.float32) + rest).astype(jnp.bfloat16) for part, rest in handed]
    return jnp.concatenate(out, axis=1)[None]


def solution(mesh):
    fine = Mesh(mesh.devices.reshape(2, NZ, NX, NY), ("segment",) + SEQ)
    in_specs = (
        P(SEQ, None),
        P("segment", SEQ, None),
        P("segment", SEQ, None),
        P("segment", SEQ, None),
        P("segment", None),
        P("segment", None),
        P("segment", SEQ, None, None),
        P(),
        P("segment", SEQ, None),
    )
    return jax.shard_map(
        per_device, mesh=fine, in_specs=in_specs, out_specs=P("segment", SEQ, None), check_vma=False
    )
```
